1024 devices in a mesh: dp: 64 (over z, core), mp: 16 (over x, y).
Axes of the slice: x: 4, y: 4, z: 32, core: 2. Of those that a mesh axis runs over, the one named last changes fastest.
Arguments:
- cotangent: bfloat16 [16384, 6144], P('dp', 'mp'), may hold values from -384 to 384
- out_weight: bfloat16 [6144, 6144], P('mp', 'dp'), may hold values from -0.078125 to 0.078125
- queries: bfloat16 [16384, 6144], P('dp', 'mp'), may hold values from -2 to 2
- keys: bfloat16 [16384, 6144], P('dp', 'mp'), may hold values from -2 to 2
- values: bfloat16 [16384, 6144], P('dp', 'mp'), may hold values from -6 to 6
- image_loss: float32 [64], P('dp'), may hold values from 0.3 to 4.5
- group_ids: int32 [64], P('dp'), may hold values from 0 to 31
- group_weights: float32 [32], replicated, may hold values from 0.2 to 1
Outputs:
- query_grad: bfloat16 [16384, 6144], P('dp', 'mp')
- key_grad: bfloat16 [16384, 6144], P('dp', 'mp')
- value_grad: bfloat16 [16384, 6144], P('dp', 'mp')
- new_weights: float32 [32], replicated
The draws below stay inside these ranges and needn't reach their ends.
All inputs are finite; a program needn't handle non-finite values.
Results may differ from the reference program's by a relative error of at most 0.0058.
Values may be sent and summed in bfloat16 or wider, within the bound.
No kernel may reach another device: no remote copies, remote signals or barrier semaphores. Data moves between devices by JAX's collectives and lax.ppermute only.
A program may use at most 32 MiB of HBM per device.

```python
import math
import jax
import jax.numpy as jnp
from jax import lax

D = 6144
HEADS = 48
HD = 128
PATCHES = 256
GROUPS = 32
IMAGES = 64
TOKENS = 16384


def draw_image_loss(key, part):
    key = jax.random.fold_in(key, 7)
    position = jnp.arange(IMAGES, dtype=jnp.float32) / (IMAGES - 1)
    noise = jax.random.uniform(key, (IMAGES,), jnp.float32, 0.5, 1.5)
    ramp = 1.0 + 2.0 * position
    return noise * ramp


def place_ends(result, rng, least, high):
    longest = result.shape.index(max(result.shape))
    spots = []
    for shift in (0, 1):
        where = [jax.random.randint(jax.random.fold_in(rng, axis), (), 0, length) for axis, length in enumerate(result.shape)]
        where[longest] = (where[longest] + shift) % result.shape[longest]
        spots.append(tuple(where))
    return result.at[spots[0]].set(least).at[spots[1]].set(high)


def block_levels(own_key, shape, shards, low, top_value):
    factor_of = 1.0
    for dim, shards_of in shards:
        heights = jax.random.uniform(jax.random.fold_in(jax.random.fold_in(own_key, 6), dim), (shards_of,), jnp.float32, low / len(shards), top_value / len(shards))
        factor_of = factor_of * jnp.repeat(jnp.exp(heights), shape[dim] // shards_of).reshape((-1,) + (1,) * (len(shape) - 1 - dim))
    return factor_of


def bell_draw(stream_key, shape, scale, limit, pieces=(), held_as=jnp.bfloat16):
    array = jax.random.normal(stream_key, shape, jnp.float32) * scale
    if len(pieces) > 0:
        array = block_levels(stream_key, shape, pieces, -0.22, 0.18) * array
    return jnp.clip(array, min=-limit, max=limit).astype(held_as)


def setup_inputs(seed: int = 0) -> dict:
    key_list = jax.random.split(jax.random.key(seed), 9)
    cotangent = bell_draw(key_list[0], (TOKENS, D), 64.0, 384.0, ((0, 64), (1, 16)))
    out_weight = bell_draw(key_list[1], (D, D), D ** -0.5, 0.078125, ((0, 16), (1, 64)))
    queries = jnp.clip(jax.random.uniform(key_list[2], (TOKENS, D), jnp.float32, -2.0, 2.0) * block_levels(key_list[2], (TOKENS, D), ((0, 64), (1, 16)), -0.4, 0.0), -2.0, 2.0).astype(jnp.bfloat16)
    keys = jnp.clip(jax.random.uniform(key_list[3], (TOKENS, D), jnp.float32, -2.0, 2.0) * block_levels(key_list[3], (TOKENS, D), ((0, 64), (1, 16)), -0.4, 0.0), -2.0, 2.0).astype(jnp.bfloat16)
    values = bell_draw(key_list[4], (TOKENS, D), 1.0, 6.0, ((0, 64), (1, 16)))
    image_loss = draw_image_loss(jax.random.fold_in(key_list[8], 71), 0)
    group_ids = place_ends(jax.random.randint(key_list[6], (IMAGES,), 0, GROUPS), jax.random.fold_in(key_list[6], 1), 0, GROUPS - 1).astype(jnp.int32)
    group_weights = jnp.clip(jnp.exp(jax.random.uniform(key_list[7], (GROUPS,), jnp.float32, math.log(0.2), math.log(1.0))), 0.2, 1.0)
    return dict(cotangent=cotangent, out_weight=out_weight, queries=queries, keys=keys, values=values, image_loss=image_loss, group_ids=group_ids, group_weights=group_weights)


robust_rate = 0.5

def image_backward(block):
    query, key_block, value, grad = block
    query_f = query.astype(jnp.float32)
    key_f = key_block.astype(jnp.float32)
    value_f = value.astype(jnp.float32)
    grad_f = grad.astype(jnp.float32)
    factor = 1.0 / jnp.sqrt(jnp.float32(HD))
    scores = jnp.einsum('phd,qhd->hpq', query_f, key_f) * factor
    raised = jnp.exp(scores)
    probs = raised / lax.optimization_barrier(jnp.sum(raised, axis=-1, keepdims=True))
    probs_low = lax.optimization_barrier(probs.astype(jnp.bfloat16)).astype(jnp.float32)
    value_grad = jnp.einsum('hpq,phd->qhd', probs_low, grad_f).astype(jnp.bfloat16)
    prob_grad = jnp.einsum('phd,qhd->hpq', grad_f, value_f)
    centre = lax.optimization_barrier(jnp.sum(probs * prob_grad, axis=-1, keepdims=True))
    score_low = lax.optimization_barrier((probs * (prob_grad - centre)).astype(jnp.bfloat16)).astype(jnp.float32)
    query_grad = (jnp.einsum('hpq,qhd->phd', score_low, key_f) * factor).astype(jnp.bfloat16)
    key_grad = (jnp.einsum('hpq,phd->qhd', score_low, query_f) * factor).astype(jnp.bfloat16)
    return (query_grad, key_grad, value_grad)

def reference(cotangent, out_weight, queries, keys, values, image_loss, group_ids, group_weights):
    labels = jnp.arange(GROUPS, dtype=jnp.int32)
    member = (group_ids[:, None] == labels[None, :]).astype(jnp.float32)
    counts = lax.optimization_barrier(jnp.sum(member, axis=0))
    totals = lax.optimization_barrier(jnp.sum(member * image_loss[:, None], axis=0))
    floored = jnp.maximum(counts, 1.0)
    raised = group_weights * jnp.exp(robust_rate * (totals / floored))
    new_weights = raised / jnp.sum(raised)
    image_scale = lax.optimization_barrier(jnp.sum(member * (new_weights / floored)[None, :], axis=1))
    product = jnp.dot(cotangent, out_weight.T, preferred_element_type=jnp.float32)
    row_scale = jnp.repeat(image_scale, PATCHES, total_repeat_length=TOKENS)
    head_grad = (product * row_scale[:, None]).astype(jnp.bfloat16)
    shape4 = (IMAGES, PATCHES, HEADS, HD)
    query_grad, key_grad, value_grad = lax.map(image_backward, (queries.reshape(shape4), keys.reshape(shape4), values.reshape(shape4), head_grad.reshape(shape4)))
    return (query_grad.reshape(TOKENS, D), key_grad.reshape(TOKENS, D), value_grad.reshape(TOKENS, D), new_weights)
```

```python
import functools

import jax
import jax.numpy as jnp
from jax import lax
from jax.experimental import pallas as pl
from jax.experimental.pallas import tpu as pltpu
from jax.sharding import PartitionSpec as P

HD = 128
PATCHES = 256
ROBUST_RATE = 0.5
SIDE = 4
FAR = 8
UNIT = 96
STATS = 4
ALL = ("dp", "mp")


def along_z(x, step0, step1, pairs_z):
    pairs = [
        (2 * z + c, 2 * ((z + step) % pairs_z) + c)
        for z in range(pairs_z)
        for c, step in ((0, step0), (1, step1))
    ]
    return lax.ppermute(x, "dp", pairs)


def to_sibling(x, pairs_z):
    return lax.ppermute(x, "dp", [(i, i ^ 1) for i in range(2 * pairs_z)])


def in_plane(x, step, first_axis, pairs_z):
    pairs = []
    for d in range(2 * pairs_z):
        on_x = (d % 2 == 0) == first_axis
        for m in range(SIDE * SIDE):
            i, j = divmod(m, SIDE)
            if on_x:
                i = (i + step) % SIDE
            else:
                j = (j + step) % SIDE
            pairs.append((d * SIDE * SIDE + m, d * SIDE * SIDE + i * SIDE + j))
    return lax.ppermute(x, ALL, pairs)


def ring_of_four(block, first_axis, pairs_z):
    half = block.shape[0] // 2
    ahead = in_plane(block, 1, first_axis, pairs_z)
    back = in_plane(block, -1, first_axis, pairs_z)
    ahead2 = in_plane(ahead[:half], 1, first_axis, pairs_z)
    back2 = in_plane(back[half:], -1, first_axis, pairs_z)
    return jnp.concatenate([block, ahead, ahead2, back2, back])


def gather_weight(unit, first, pairs_z):
    other = to_sibling(unit, pairs_z)
    chip = jnp.concatenate([jnp.where(first, unit, other), jnp.where(first, other, unit)])
    got = along_z(chip, FAR, -FAR, pairs_z)
    rows = unit.shape[0]
    got0, got1 = got[:rows], got[rows:]
    mine = jnp.where(first, got0, got1)
    opposite = to_sibling(jnp.where(first, got1, got0), pairs_z)
    farthest = along_z(mine, FAR, -FAR, pairs_z)
    held = (unit, opposite, farthest, mine)
    bundle = jnp.concatenate([h[:UNIT] for h in held] + [h[UNIT:] for h in held])
    pieces = [bundle]
    p = q = bundle
    for _ in range(FAR // 2 - 1):
        p = along_z(p, 1, -1, pairs_z)
        q = along_z(q, -1, 1, pairs_z)
        pieces += [p, q]
    p = along_z(jnp.concatenate([p[: 2 * UNIT], p[4 * UNIT :]]), 1, -1, pairs_z)
    q = along_z(jnp.concatenate([q[UNIT : 3 * UNIT], q[4 * UNIT :]]), -1, 1, pairs_z)
    return pieces + [p, q]


def piece_offsets():
    slots = [0, FAR, 2 * FAR, -FAR]
    offsets = [slots]
    for k in range(1, FAR // 2):
        offsets += [[o - k for o in slots], [o + k for o in slots]]
    k = FAR // 2
    offsets += [[o - k for o in slots[:2]], [o + k for o in slots[1:3]]]
    return offsets


def matmul_kernel(starts, core, x_ref, *refs):
    pieces, (mine_ref, send_ref, xs_ref, acc_ref) = refs[:9], refs[9:]
    slot = 0
    stats = jnp.zeros((16, mine_ref.shape[1]), jnp.float32)
    row = lax.broadcasted_iota(jnp.int32, stats.shape, 0)
    for i, piece in enumerate(pieces):
        units = 4 if i < 7 else 2
        depth = units * UNIT
        for k in range(units):
            at = pl.multiple_of(starts[slot], 32)
            xs_ref[pl.ds(k * UNIT, UNIT), :] = x_ref[pl.ds(at, UNIT), :]
            slot += 1
        product = lax.dot_general(
            xs_ref[pl.ds(0, depth), :],
            piece[pl.ds(0, depth), :],
            (((0,), (0,)), ((), ())),
            preferred_element_type=jnp.float32,
        )
        if i == 0:
            acc_ref[...] = product
        else:
            acc_ref[...] += product
        extra = piece[pl.ds(depth, 16), :].astype(jnp.float32)
        if i == 7:
            extra = jnp.where(row < 8, extra, 0.0)
        if i == 8:
            extra = jnp.where((row >= 4) & (row < 12), extra, 0.0)
        stats += extra
    count = jnp.sum(jnp.where(row % 4 == 0, stats, 0.0), axis=0, keepdims=True)
    total = jnp.sum(jnp.where(row % 4 == 0, 0.0, stats), axis=0, keepdims=True)
    row8 = row[:8]
    tail = jnp.where(row8 == 0, count, jnp.where(row8 == 1, total, 0.0))
    here = pl.multiple_of(core[0] * PATCHES, PATCHES)
    there = pl.multiple_of((1 - core[0]) * PATCHES, PATCHES)
    mine_ref[pl.ds(0, PATCHES), :] = acc_ref[pl.ds(here, PATCHES), :]
    send_ref[pl.ds(0, PATCHES), :] = acc_ref[pl.ds(there, PATCHES), :]
    mine_ref[pl.ds(PATCHES, 8), :] = tail
    send_ref[pl.ds(PATCHES, 8), :] = tail


def attention_kernel(group, mine_ref, got_ref, gw_ref, q_ref, k_ref, v_ref, dq_ref, dk_ref, dv_ref, nw_ref):
    f32, bf16 = jnp.float32, jnp.bfloat16
    width = gw_ref.shape[1]
    tail = mine_ref[pl.ds(PATCHES, 8), :width] + got_ref[pl.ds(PATCHES, 8), :width]
    counts, totals = tail[0:1], tail[1:2]
    floored = jnp.maximum(counts, 1.0)
    raised = gw_ref[...] * jnp.exp(ROBUST_RATE * (totals / floored))
    new_weights = raised / jnp.sum(raised, axis=1, keepdims=True)
    nw_ref[...] = new_weights
    label = lax.broadcasted_iota(jnp.int32, (1, width), 1)
    scale = jnp.sum(
        jnp.where(label == group[0], new_weights / floored, 0.0), axis=1, keepdims=True
    )
    product = mine_ref[pl.ds(0, PATCHES), :] + got_ref[pl.ds(0, PATCHES), :]
    head_grad = (product * scale).astype(bf16)
    factor = 1.0 / jnp.sqrt(f32(HD))
    rows_by_rows = (((1,), (1,)), ((), ()))
    columns = (((0,), (0,)), ((), ()))
    plain = (((1,), (0,)), ((), ()))
    dot = functools.partial(lax.dot_general, preferred_element_type=f32)
    for h in range(q_ref.shape[1] // HD):
        cols = slice(h * HD, (h + 1) * HD)
        q, k, v, g = q_ref[:, cols], k_ref[:, cols], v_ref[:, cols], head_grad[:, cols]
        raised_scores = jnp.exp(dot(q, k, rows_by_rows) * factor)
        probs = raised_scores / jnp.sum(raised_scores, axis=1, keepdims=True)
        dv_ref[:, cols] = dot(probs.astype(bf16), g, columns).astype(bf16)
        prob_grad = dot(g, v, rows_by_rows)
        centre = jnp.sum(probs * prob_grad, axis=1, keepdims=True)
        score = (probs * (prob_grad - centre)).astype(bf16)
        dq_ref[:, cols] = (dot(score, k, plain) * factor).astype(bf16)
        dk_ref[:, cols] = (dot(score, q, columns) * factor).astype(bf16)


VM = pl.BlockSpec(memory_space=pltpu.VMEM)
SM = pl.BlockSpec(memory_space=pltpu.SMEM)


def per_device(pairs_z, cotangent, out_weight, queries, keys, values, image_loss, group_ids, group_weights):
    f32, bf16 = jnp.float32, jnp.bfloat16
    groups = group_weights.shape[0]
    heads = queries.shape[1]
    core = lax.axis_index("dp") % 2
    first = core == 0
    z = lax.axis_index("dp") // 2
    mp = lax.axis_index("mp")
    at_x, at_y = mp // SIDE, mp % SIDE

    loss = image_loss[0]
    high = lax.reduce_precision(loss, 8, 7)
    middle = lax.reduce_precision(loss - high, 8, 7)
    low = loss - high - middle
    member = (jnp.arange(heads) == group_ids[0]).astype(f32)
    stats = jnp.stack([member, member * high, member * middle, member * low]).astype(bf16)
    unit = jnp.concatenate([out_weight.T, stats])
    pieces = gather_weight(unit, first, pairs_z)

    turned = cotangent.T.reshape(2, 2, UNIT, PATCHES)
    keep = jnp.where(first, turned[:, 0], turned[:, 1])
    give = jnp.where(first, turned[:, 1], turned[:, 0])
    got = to_sibling(give, pairs_z)
    block = jnp.concatenate([jnp.where(first, keep, got), jnp.where(first, got, keep)], axis=2)
    block = block.reshape(2 * UNIT, 2 * PATCHES)
    block = ring_of_four(block, True, pairs_z)
    features = ring_of_four(block, False, pairs_z)

    offsets = jnp.array([o for piece in piece_offsets() for o in piece], jnp.int32)
    source = (z + jnp.where(first, offsets, -offsets)) % pairs_z
    from_x, from_y = (at_x - source // 2 // SIDE) % SIDE, (at_y - source // 2 % SIDE) % SIDE
    inner = jnp.where(first, from_x, from_y)
    outer = jnp.where(first, from_y, from_x)
    starts = ((outer * SIDE + inner) * 2 + source % 2) * UNIT

    rows = PATCHES + 8
    partial = jax.ShapeDtypeStruct((rows, heads), f32)
    mine, send = pl.pallas_call(
        matmul_kernel,
        out_shape=(partial, partial),
        in_specs=[SM, SM] + [VM] * 10,
        out_specs=(VM, VM),
        scratch_shapes=[
            pltpu.VMEM((4 * UNIT, 2 * PATCHES), bf16),
            pltpu.VMEM((2 * PATCHES, heads), f32),
        ],
        compiler_params=pltpu.CompilerParams(vmem_limit_bytes=40 * 2**20),
        cost_estimate=pl.CostEstimate(
            flops=2 * 512 * 3072 * heads, bytes_accessed=7 * 2**20, transcendentals=0
        ),
        name="project",
    )(starts, core.reshape(1), features, *pieces)
    received = to_sibling(send, pairs_z)

    width = 128
    grown = jnp.pad(group_weights, (0, width - groups)).reshape(1, width)
    out = jax.ShapeDtypeStruct(queries.shape, bf16)
    query_grad, key_grad, value_grad, new_weights = pl.pallas_call(
        attention_kernel,
        out_shape=(out, out, out, jax.ShapeDtypeStruct((1, width), f32)),
        in_specs=[SM] + [VM] * 6,
        out_specs=(VM,) * 4,
        compiler_params=pltpu.CompilerParams(vmem_limit_bytes=40 * 2**20),
        cost_estimate=pl.CostEstimate(
            flops=10 * 256 * 256 * heads, bytes_accessed=2 * 2**20, transcendentals=3 * 65536
        ),
        name="attention",
    )(group_ids, mine, received, grown, queries, keys, values)
    return query_grad, key_grad, value_grad, new_weights[0, :groups]


def solution(mesh):
    placed = (
        P("dp", "mp"),
        P("mp", "dp"),
        P("dp", "mp"),
        P("dp", "mp"),
        P("dp", "mp"),
        P("dp"),
        P("dp"),
        P(),
    )
    return jax.shard_map(
        functools.partial(per_device, mesh.shape["dp"] // 2),
        mesh=mesh,
        in_specs=placed,
        out_specs=(P("dp", "mp"), P("dp", "mp"), P("dp", "mp"), P()),
        check_vma=False,
    )
```

```python
import functools

import jax
import jax.numpy as jnp
from jax import lax
from jax.experimental import pallas as pl
from jax.experimental.pallas import tpu as pltpu
from jax.sharding import PartitionSpec as P

HD = 128
PATCHES = 256
ROBUST_RATE = 0.5
SIDE = 4
FAR = 8
UNIT = 96
STATS = 4
TAIL = 16
ALL = ("dp", "mp")


def along_z(x, step0, step1, pairs_z):
    pairs = [
        (2 * z + c, 2 * ((z + step) % pairs_z) + c)
        for z in range(pairs_z)
        for c, step in ((0, step0), (1, step1))
    ]
    return lax.ppermute(x, "dp", pairs)


def to_sibling(x, pairs_z):
    return lax.ppermute(x, "dp", [(i, i ^ 1) for i in range(2 * pairs_z)])


def in_plane(x, step, first_axis, pairs_z):
    pairs = []
    for d in range(2 * pairs_z):
        on_x = (d % 2 == 0) == first_axis
        for m in range(SIDE * SIDE):
            i, j = divmod(m, SIDE)
            if on_x:
                i = (i + step) % SIDE
            else:
                j = (j + step) % SIDE
            pairs.append((d * SIDE * SIDE + m, d * SIDE * SIDE + i * SIDE + j))
    return lax.ppermute(x, ALL, pairs)


def ring_of_four(block, first_axis, pairs_z):
    return [block] + [in_plane(block, step, first_axis, pairs_z) for step in (1, 2, -1)]


def gather_weight(unit, other, first, pairs_z):
    chip = jnp.concatenate([jnp.where(first, unit, other), jnp.where(first, other, unit)])
    got = along_z(chip, FAR, -FAR, pairs_z)
    rows = unit.shape[0]
    got0, got1 = got[:rows], got[rows:]
    mine = jnp.where(first, got0, got1)
    farthest = along_z(mine, FAR, -FAR, pairs_z)
    opposite = to_sibling(jnp.where(first, got1, got0), pairs_z)
    bundle = join_units(unit, opposite, farthest, mine)
    pieces = [bundle]
    p = q = bundle
    for _ in range(FAR // 2 - 1):
        p = along_z(p, 1, -1, pairs_z)
        q = along_z(q, -1, 1, pairs_z)
        pieces += [p, q]
    p = along_z(jnp.concatenate([p[: 2 * UNIT], p[4 * UNIT :]]), 1, -1, pairs_z)
    q = along_z(jnp.concatenate([q[UNIT : 3 * UNIT], q[4 * UNIT :]]), -1, 1, pairs_z)
    return pieces + [p, q]


def piece_offsets():
    slots = [0, FAR, 2 * FAR, -FAR]
    offsets = [slots]
    for k in range(1, FAR // 2):
        offsets += [[o - k for o in slots], [o + k for o in slots]]
    k = FAR // 2
    offsets += [[o - k for o in slots[:2]], [o + k for o in slots[1:3]]]
    return offsets


def unit_kernel(group, loss, weight_ref, unit_ref):
    heads = weight_ref.shape[1]
    unit_ref[pl.ds(0, UNIT), :] = weight_ref[...]
    x = jnp.full((TAIL, heads), loss[0], jnp.float32)
    high = x.astype(jnp.bfloat16).astype(jnp.float32)
    middle = (x - high).astype(jnp.bfloat16).astype(jnp.float32)
    low = x - high - middle
    row = lax.broadcasted_iota(jnp.int32, x.shape, 0)
    lane = lax.broadcasted_iota(jnp.int32, x.shape, 1)
    value = jnp.where(row == 0, 1.0, jnp.where(row == 1, high, jnp.where(row == 2, middle, low)))
    value = jnp.where((row < STATS) & (lane == group[0]), value, 0.0)
    unit_ref[pl.ds(UNIT, TAIL), :] = value.astype(jnp.bfloat16)


def join_kernel(*refs):
    *units, out = refs
    tail = jnp.zeros((TAIL, out.shape[1]), jnp.float32)
    for i, ref in enumerate(units):
        out[pl.ds(i * UNIT, UNIT), :] = ref[pl.ds(0, UNIT), :]
        rows = ref[pl.ds(UNIT, TAIL), :].astype(jnp.float32)
        tail += pltpu.roll(rows, STATS * i, 0) if i else rows
    out[pl.ds(len(units) * UNIT, TAIL), :] = tail.astype(jnp.bfloat16)


def stack_kernel(*refs):
    *blocks, out = refs
    rows = blocks[0].shape[0]
    for i, ref in enumerate(blocks):
        out[pl.ds(i * rows, rows), :] = ref[...]


def scores_kernel(q_ref, k_ref, probs_ref):
    factor = 1.0 / jnp.sqrt(jnp.float32(HD))
    for h in range(q_ref.shape[1] // HD):
        cols = slice(h * HD, (h + 1) * HD)
        scores = lax.dot_general(
            q_ref[:, cols],
            k_ref[:, cols],
            (((1,), (1,)), ((), ())),
            preferred_element_type=jnp.float32,
        )
        raised = jnp.exp(scores * factor)
        probs_ref[h] = raised / jnp.sum(raised, axis=1, keepdims=True)


def pick_rows(starts, outers, slot, blocks, xs_ref, at):
    row = pl.multiple_of(starts[slot], 32)
    for i, block in enumerate(blocks):

        @pl.when(outers[slot] == i)
        def _():
            xs_ref[pl.ds(at, UNIT), :] = block[pl.ds(row, UNIT), :]


def product_of(xs, weight):
    return lax.dot_general(
        xs, weight, (((0,), (0,)), ((), ())), preferred_element_type=jnp.float32
    )


def first_kernel(starts, outers, *refs):
    blocks, pieces, (acc_ref, stats_ref, xs_ref) = refs[:4], refs[4:-3], refs[-3:]
    depth = 4 * UNIT
    stats_ref[...] = jnp.zeros_like(stats_ref)
    for i, piece in enumerate(pieces):
        for k in range(4):
            pick_rows(starts, outers, 4 * i + k, blocks, xs_ref, k * UNIT)
        product = product_of(xs_ref[...], piece[pl.ds(0, depth), :])
        if i == 0:
            acc_ref[...] = product
        else:
            acc_ref[...] += product
        stats_ref[...] += piece[pl.ds(depth, TAIL), :].astype(jnp.float32)


def last_kernel(starts, outers, core, *refs):
    blocks, (p_ref, q_ref, acc_ref, stats_ref, mine_ref, send_ref, xs_ref, w_ref, sum_ref) = refs[:4], refs[4:]
    depth = 2 * UNIT
    for k in range(4):
        pick_rows(starts, outers, 28 + k, blocks, xs_ref, k * UNIT)
    w_ref[pl.ds(0, depth), :] = p_ref[pl.ds(0, depth), :]
    w_ref[pl.ds(depth, depth), :] = q_ref[pl.ds(0, depth), :]
    sum_ref[...] = acc_ref[...] + product_of(xs_ref[...], w_ref[...])
    stats = stats_ref[...]
    row = lax.broadcasted_iota(jnp.int32, stats.shape, 0)
    stats += jnp.where(row < 8, p_ref[pl.ds(depth, TAIL), :].astype(jnp.float32), 0.0)
    middle = (row >= 4) & (row < 12)
    stats += jnp.where(middle, q_ref[pl.ds(depth, TAIL), :].astype(jnp.float32), 0.0)
    count = jnp.sum(jnp.where(row % 4 == 0, stats, 0.0), axis=0, keepdims=True)
    total = jnp.sum(jnp.where(row % 4 == 0, 0.0, stats), axis=0, keepdims=True)
    row8 = row[:8]
    tail = jnp.where(row8 == 0, count, jnp.where(row8 == 1, total, 0.0))
    here = pl.multiple_of(core[0] * PATCHES, PATCHES)
    there = pl.multiple_of((1 - core[0]) * PATCHES, PATCHES)
    mine_ref[pl.ds(0, PATCHES), :] = sum_ref[pl.ds(here, PATCHES), :]
    send_ref[pl.ds(0, PATCHES), :] = sum_ref[pl.ds(there, PATCHES), :]
    mine_ref[pl.ds(PATCHES, 8), :] = tail
    send_ref[pl.ds(PATCHES, 8), :] = tail


def attention_kernel(group, mine_ref, got_ref, gw_ref, probs_ref, q_ref, k_ref, v_ref, dq_ref, dk_ref, dv_ref, nw_ref):
    f32, bf16 = jnp.float32, jnp.bfloat16
    width = gw_ref.shape[1]
    tail = mine_ref[pl.ds(PATCHES, 8), :] + got_ref[pl.ds(PATCHES, 8), :]
    counts, totals = tail[0:1, :width], tail[1:2, :width]
    floored = jnp.maximum(counts, 1.0)
    raised = gw_ref[...] * jnp.exp(ROBUST_RATE * (totals / floored))
    new_weights = raised / jnp.sum(raised, axis=1, keepdims=True)
    nw_ref[...] = new_weights
    label = lax.broadcasted_iota(jnp.int32, (1, width), 1)
    scale = jnp.sum(
        jnp.where(label == group[0], new_weights / floored, 0.0), axis=1, keepdims=True
    )
    product = mine_ref[pl.ds(0, PATCHES), :] + got_ref[pl.ds(0, PATCHES), :]
    head_grad = (product * scale).astype(bf16)
    factor = 1.0 / jnp.sqrt(f32(HD))
    rows_by_rows = (((1,), (1,)), ((), ()))
    columns = (((0,), (0,)), ((), ()))
    plain = (((1,), (0,)), ((), ()))
    dot = functools.partial(lax.dot_general, preferred_element_type=f32)
    for h in range(q_ref.shape[1] // HD):
        cols = slice(h * HD, (h + 1) * HD)
        q, k, v, g = q_ref[:, cols], k_ref[:, cols], v_ref[:, cols], head_grad[:, cols]
        probs = probs_ref[h]
        dv_ref[:, cols] = dot(probs.astype(bf16), g, columns).astype(bf16)
        prob_grad = dot(g, v, rows_by_rows)
        centre = jnp.sum(probs * prob_grad, axis=1, keepdims=True)
        score = (probs * (prob_grad - centre)).astype(bf16)
        dq_ref[:, cols] = (dot(score, k, plain) * factor).astype(bf16)
        dk_ref[:, cols] = (dot(score, q, columns) * factor).astype(bf16)


VM = pl.BlockSpec(memory_space=pltpu.VMEM)
SM = pl.BlockSpec(memory_space=pltpu.SMEM)


def call(kernel, name, out_shape, operands, scalars=0, scratch=(), flops=0, moved=2**20):
    outs = jax.tree.map(lambda _: VM, out_shape)
    return pl.pallas_call(
        kernel,
        out_shape=out_shape,
        in_specs=[SM] * scalars + [VM] * (len(operands) - scalars),
        out_specs=outs,
        scratch_shapes=scratch,
        compiler_params=pltpu.CompilerParams(vmem_limit_bytes=40 * 2**20),
        cost_estimate=pl.CostEstimate(flops=flops, bytes_accessed=moved, transcendentals=0),
        name=name,
    )(*operands)


def join_units(*units):
    rows = len(units) * UNIT + TAIL
    shape = jax.ShapeDtypeStruct((rows, units[0].shape[1]), units[0].dtype)
    return call(join_kernel, "join_units", shape, units)


def per_device(pairs_z, cotangent, out_weight, queries, keys, values, image_loss, group_ids, group_weights):
    f32, bf16 = jnp.float32, jnp.bfloat16
    groups = group_weights.shape[0]
    heads = queries.shape[1]
    core = lax.axis_index("dp") % 2
    first = core == 0
    z = lax.axis_index("dp") // 2
    mp = lax.axis_index("mp")
    at_x, at_y = mp // SIDE, mp % SIDE

    unit = call(
        unit_kernel,
        "make_unit",
        jax.ShapeDtypeStruct((UNIT + TAIL, heads), bf16),
        (group_ids, image_loss, out_weight.T),
        2,
        moved=2**17,
    )
    other = to_sibling(unit, pairs_z)

    turned = cotangent.T.reshape(2, 2, UNIT, PATCHES)
    keep = jnp.where(first, turned[:, 0], turned[:, 1])
    give = jnp.where(first, turned[:, 1], turned[:, 0])
    got = to_sibling(give, pairs_z)
    block = jnp.concatenate([jnp.where(first, keep, got), jnp.where(first, got, keep)], axis=2)
    block = block.reshape(2 * UNIT, 2 * PATCHES)
    row_of_blocks = call(
        stack_kernel,
        "stack",
        jax.ShapeDtypeStruct((8 * UNIT, 2 * PATCHES), bf16),
        ring_of_four(block, True, pairs_z),
    )
    features = ring_of_four(row_of_blocks, False, pairs_z)
    pieces = gather_weight(unit, other, first, pairs_z)

    offsets = jnp.array([o for piece in piece_offsets() for o in piece], jnp.int32)
    source = (z + jnp.where(first, offsets, -offsets)) % pairs_z
    from_x, from_y = (at_x - source // 2 // SIDE) % SIDE, (at_y - source // 2 % SIDE) % SIDE
    inner = jnp.where(first, from_x, from_y)
    outer = jnp.where(first, from_y, from_x)
    starts = (inner * 2 + source % 2) * UNIT

    total = jax.ShapeDtypeStruct((2 * PATCHES, heads), f32)
    summed, stats = call(
        first_kernel,
        "project_first",
        (total, jax.ShapeDtypeStruct((TAIL, heads), f32)),
        (starts, outer, *features, *pieces[:7]),
        2,
        [pltpu.VMEM((4 * UNIT, 2 * PATCHES), bf16)],
        2 * 512 * 2688 * heads,
        6 * 2**20,
    )
    partial = jax.ShapeDtypeStruct((PATCHES + 8, heads), f32)
    mine, send = call(
        last_kernel,
        "project_last",
        (partial, partial),
        (starts, outer, core.reshape(1), *features, *pieces[7:], summed, stats),
        3,
        [
            pltpu.VMEM((4 * UNIT, 2 * PATCHES), bf16),
            pltpu.VMEM((4 * UNIT, heads), bf16),
            pltpu.VMEM((2 * PATCHES, heads), f32),
        ],
        2 * 512 * 384 * heads,
        2 * 2**20,
    )
    received = to_sibling(send, pairs_z)

    probs = call(
        scores_kernel,
        "scores",
        jax.ShapeDtypeStruct((heads // HD, PATCHES, PATCHES), f32),
        (queries, keys),
        flops=2 * PATCHES * PATCHES * heads,
    )
    out = jax.ShapeDtypeStruct(queries.shape, bf16)
    query_grad, key_grad, value_grad, new_weights = call(
        attention_kernel,
        "attention",
        (out, out, out, jax.ShapeDtypeStruct((1, groups), f32)),
        (group_ids, mine, received, group_weights.reshape(1, groups), probs, queries, keys, values),
        1,
        flops=8 * PATCHES * PATCHES * heads,
        moved=3 * 2**20,
    )
    return query_grad, key_grad, value_grad, new_weights.reshape(groups)


def solution(mesh):
    placed = (
        P("dp", "mp"),
        P("mp", "dp"),
        P("dp", "mp"),
        P("dp", "mp"),
        P("dp", "mp"),
        P("dp"),
        P("dp"),
        P(),
    )
    return jax.shard_map(
        functools.partial(per_device, mesh.shape["dp"] // 2),
        mesh=mesh,
        in_specs=placed,
        out_specs=(P("dp", "mp"), P("dp", "mp"), P("dp", "mp"), P()),
        check_vma=False,
    )
```

```python
import functools

import jax
import jax.numpy as jnp
from jax import lax
from jax.experimental import pallas as pl
from jax.experimental.pallas import tpu as pltpu
from jax.sharding import PartitionSpec as P

HD = 128
PATCHES = 256
ROBUST_RATE = 0.5
SIDE = 4
FAR = 8
UNIT = 96
STATS = 4
TAIL = 16
HALF = 2 * UNIT + TAIL
FULL = 4 * UNIT + TAIL
ALL = ("dp", "mp")


def along_z(x, step0, step1, pairs_z):
    pairs = [
        (2 * z + c, 2 * ((z + step) % pairs_z) + c)
        for z in range(pairs_z)
        for c, step in ((0, step0), (1, step1))
    ]
    return lax.ppermute(x, "dp", pairs)


def to_sibling(x, pairs_z):
    return lax.ppermute(x, "dp", [(i, i ^ 1) for i in range(2 * pairs_z)])


def in_plane(x, step, first_axis, pairs_z):
    pairs = []
    for d in range(2 * pairs_z):
        on_x = (d % 2 == 0) == first_axis
        for m in range(SIDE * SIDE):
            i, j = divmod(m, SIDE)
            if on_x:
                i = (i + step) % SIDE
            else:
                j = (j + step) % SIDE
            pairs.append((d * SIDE * SIDE + m, d * SIDE * SIDE + i * SIDE + j))
    return lax.ppermute(x, ALL, pairs)


def ring_of_four(block, first_axis, pairs_z):
    return [block] + [in_plane(block, step, first_axis, pairs_z) for step in (1, 2, -1)]


def gather(unit, other, block, first, pairs_z):
    chip = jnp.concatenate([jnp.where(first, unit, other), jnp.where(first, other, unit)])
    got = along_z(chip, FAR, -FAR, pairs_z)
    rows = unit.shape[0]
    got0, got1 = got[:rows], got[rows:]
    mine = jnp.where(first, got0, got1)
    row = ring_of_four(block, True, pairs_z)
    mine, *row = lax.optimization_barrier((mine, *row))
    farthest = along_z(mine, FAR, -FAR, pairs_z)
    opposite = to_sibling(jnp.where(first, got1, got0), pairs_z)
    bundle = join_units(unit, opposite, farthest, mine)
    row = stack(row)
    pieces, features = [bundle], [row]
    p = q = bundle
    for step in (2, 1, -1):
        features.append(in_plane(row, step, False, pairs_z))
        p = along_z(p, 1, -1, pairs_z)
        q = along_z(q, -1, 1, pairs_z)
        row, p = lax.optimization_barrier((row, p))
        pieces += [p, q]
    p = along_z(p[:HALF], 1, -1, pairs_z)
    q = along_z(q[UNIT : UNIT + HALF], -1, 1, pairs_z)
    return pieces + [p, q], [features[i] for i in (0, 2, 1, 3)]


def piece_offsets():
    slots = [0, FAR, 2 * FAR, -FAR]
    offsets = [slots]
    for k in range(1, FAR // 2):
        offsets += [[o - k for o in slots], [o + k for o in slots]]
    k = FAR // 2
    offsets += [[o - k for o in slots[:2]], [o + k for o in slots[1:3]]]
    return offsets


def unit_kernel(group, loss, weight_ref, unit_ref):
    heads = weight_ref.shape[1]
    unit_ref[pl.ds(0, UNIT), :] = weight_ref[...]
    x = jnp.full((TAIL, heads), loss[0], jnp.float32)
    high = x.astype(jnp.bfloat16).astype(jnp.float32)
    middle = (x - high).astype(jnp.bfloat16).astype(jnp.float32)
    low = x - high - middle
    row = lax.broadcasted_iota(jnp.int32, x.shape, 0)
    lane = lax.broadcasted_iota(jnp.int32, x.shape, 1)
    value = jnp.where(row == 0, 1.0, jnp.where(row == 1, high, jnp.where(row == 2, middle, low)))
    value = jnp.where((row < STATS) & (lane == group[0]), value, 0.0)
    unit_ref[pl.ds(UNIT, TAIL), :] = value.astype(jnp.bfloat16)


def join_kernel(*refs):
    *units, out = refs
    tail = jnp.zeros((TAIL, out.shape[1]), jnp.float32)
    for i, ref in enumerate(units):
        out[pl.ds(row_of(i), UNIT), :] = ref[pl.ds(0, UNIT), :]
        rows = ref[pl.ds(UNIT, TAIL), :].astype(jnp.float32)
        tail += pltpu.roll(rows, STATS * i, 0) if i else rows
    out[pl.ds(2 * UNIT, TAIL), :] = tail.astype(jnp.bfloat16)


def row_of(i):
    return i * UNIT + (TAIL if i >= 2 else 0)


def stack_kernel(*refs):
    *blocks, out = refs
    rows = blocks[0].shape[0]
    for i, ref in enumerate(blocks):
        out[pl.ds(i * rows, rows), :] = ref[...]


def scores_kernel(q_ref, k_ref, gw_ref, probs_ref, weights_ref):
    weights_ref[...] = gw_ref[...]
    factor = 1.0 / jnp.sqrt(jnp.float32(HD))
    for h in range(q_ref.shape[1] // HD):
        cols = slice(h * HD, (h + 1) * HD)
        scores = lax.dot_general(
            q_ref[:, cols],
            k_ref[:, cols],
            (((1,), (1,)), ((), ())),
            preferred_element_type=jnp.float32,
        )
        raised = jnp.exp(scores * factor)
        probs_ref[h] = raised / jnp.sum(raised, axis=1, keepdims=True)


def pick_rows(starts, outers, slot, blocks, xs_ref, at):
    row = pl.multiple_of(starts[slot], 32)
    for i, block in enumerate(blocks):

        @pl.when(outers[slot] == i)
        def _():
            xs_ref[pl.ds(at, UNIT), :] = block[pl.ds(row, UNIT), :]


def product_of(xs, weight):
    return lax.dot_general(
        xs, weight, (((0,), (0,)), ((), ())), preferred_element_type=jnp.float32
    )


def first_kernel(starts, outers, *refs):
    blocks, pieces, (acc_ref, stats_ref, xs_ref) = refs[:4], refs[4:-3], refs[-3:]
    xs_ref[pl.ds(2 * UNIT, TAIL), :] = jnp.zeros((TAIL, xs_ref.shape[1]), xs_ref.dtype)
    stats_ref[...] = jnp.zeros_like(stats_ref)
    for i, piece in enumerate(pieces):
        for k in range(4):
            pick_rows(starts, outers, 4 * i + k, blocks, xs_ref, row_of(k))
        product = product_of(xs_ref[...], piece[...])
        if i == 0:
            acc_ref[...] = product
        else:
            acc_ref[...] += product
        stats_ref[...] += piece[pl.ds(2 * UNIT, TAIL), :].astype(jnp.float32)


def last_kernel(starts, outers, core, *refs):
    blocks, (p_ref, q_ref, acc_ref, stats_ref, mine_ref, send_ref, xs_ref, w_ref, sum_ref) = refs[:4], refs[4:]
    for k, at in enumerate((0, UNIT, HALF, HALF + UNIT + TAIL)):
        pick_rows(starts, outers, 28 + k, blocks, xs_ref, at)
    for at in (2 * UNIT, HALF + UNIT):
        xs_ref[pl.ds(at, TAIL), :] = jnp.zeros((TAIL, xs_ref.shape[1]), xs_ref.dtype)
    w_ref[pl.ds(0, HALF), :] = p_ref[...]
    w_ref[pl.ds(HALF, HALF), :] = q_ref[...]
    sum_ref[...] = acc_ref[...] + product_of(xs_ref[...], w_ref[...])
    stats = stats_ref[...]
    row = lax.broadcasted_iota(jnp.int32, stats.shape, 0)
    stats += jnp.where(row < 8, p_ref[pl.ds(2 * UNIT, TAIL), :].astype(jnp.float32), 0.0)
    middle = (row >= 4) & (row < 12)
    stats += jnp.where(middle, q_ref[pl.ds(UNIT, TAIL), :].astype(jnp.float32), 0.0)
    count = jnp.sum(jnp.where(row % 4 == 0, stats, 0.0), axis=0, keepdims=True)
    total = jnp.sum(jnp.where(row % 4 == 0, 0.0, stats), axis=0, keepdims=True)
    row8 = row[:8]
    tail = jnp.where(row8 == 0, count, jnp.where(row8 == 1, total, 0.0))
    here = pl.multiple_of(core[0] * PATCHES, PATCHES)
    there = pl.multiple_of((1 - core[0]) * PATCHES, PATCHES)
    mine_ref[pl.ds(0, PATCHES), :] = sum_ref[pl.ds(here, PATCHES), :]
    send_ref[pl.ds(0, PATCHES), :] = sum_ref[pl.ds(there, PATCHES), :]
    mine_ref[pl.ds(PATCHES, 8), :] = tail
    send_ref[pl.ds(PATCHES, 8), :] = tail


def attention_kernel(group, mine_ref, got_ref, gw_ref, probs_ref, q_ref, k_ref, v_ref, dq_ref, dk_ref, dv_ref, nw_ref):
    f32, bf16 = jnp.float32, jnp.bfloat16
    width = gw_ref.shape[1]
    tail = mine_ref[pl.ds(PATCHES, 8), :] + got_ref[pl.ds(PATCHES, 8), :]
    counts, totals = tail[0:1, :width], tail[1:2, :width]
    floored = jnp.maximum(counts, 1.0)
    raised = gw_ref[...] * jnp.exp(ROBUST_RATE * (totals / floored))
    new_weights = raised / jnp.sum(raised, axis=1, keepdims=True)
    nw_ref[...] = new_weights
    label = lax.broadcasted_iota(jnp.int32, (1, width), 1)
    scale = jnp.sum(
        jnp.where(label == group[0], new_weights / floored, 0.0), axis=1, keepdims=True
    )
    product = mine_ref[pl.ds(0, PATCHES), :] + got_ref[pl.ds(0, PATCHES), :]
    head_grad = (product * scale).astype(bf16)
    factor = 1.0 / jnp.sqrt(f32(HD))
    rows_by_rows = (((1,), (1,)), ((), ()))
    columns = (((0,), (0,)), ((), ()))
    plain = (((1,), (0,)), ((), ()))
    dot = functools.partial(lax.dot_general, preferred_element_type=f32)
    for h in range(q_ref.shape[1] // HD):
        cols = slice(h * HD, (h + 1) * HD)
        q, k, v, g = q_ref[:, cols], k_ref[:, cols], v_ref[:, cols], head_grad[:, cols]
        probs = probs_ref[h]
        dv_ref[:, cols] = dot(probs.astype(bf16), g, columns).astype(bf16)
        prob_grad = dot(g, v, rows_by_rows)
        centre = jnp.sum(probs * prob_grad, axis=1, keepdims=True)
        score = (probs * (prob_grad - centre)).astype(bf16)
        dq_ref[:, cols] = (dot(score, k, plain) * factor).astype(bf16)
        dk_ref[:, cols] = (dot(score, q, columns) * factor).astype(bf16)


VM = pl.BlockSpec(memory_space=pltpu.VMEM)
SM = pl.BlockSpec(memory_space=pltpu.SMEM)


def call(kernel, name, out_shape, operands, scalars=0, scratch=(), flops=0, moved=2**20):
    outs = jax.tree.map(lambda _: VM, out_shape)
    return pl.pallas_call(
        kernel,
        out_shape=out_shape,
        in_specs=[SM] * scalars + [VM] * (len(operands) - scalars),
        out_specs=outs,
        scratch_shapes=scratch,
        compiler_params=pltpu.CompilerParams(vmem_limit_bytes=16 * 2**20),
        cost_estimate=pl.CostEstimate(flops=flops, bytes_accessed=moved, transcendentals=0),
        name=name,
    )(*operands)


def join_units(*units):
    shape = jax.ShapeDtypeStruct((FULL, units[0].shape[1]), units[0].dtype)
    return call(join_kernel, "join_units", shape, units)


def stack(blocks):
    rows, width = blocks[0].shape
    shape = jax.ShapeDtypeStruct((len(blocks) * rows, width), blocks[0].dtype)
    return call(stack_kernel, "stack", shape, blocks)


def per_device(pairs_z, cotangent, out_weight, queries, keys, values, image_loss, group_ids, group_weights):
    f32, bf16 = jnp.float32, jnp.bfloat16
    groups = group_weights.shape[0]
    heads = queries.shape[1]
    core = lax.axis_index("dp") % 2
    first = core == 0
    z = lax.axis_index("dp") // 2
    mp = lax.axis_index("mp")
    at_x, at_y = mp // SIDE, mp % SIDE

    unit = call(
        unit_kernel,
        "make_unit",
        jax.ShapeDtypeStruct((UNIT + TAIL, heads), bf16),
        (group_ids, image_loss, out_weight.T),
        2,
        moved=2**17,
    )
    other = to_sibling(unit, pairs_z)

    turned = cotangent.T.reshape(2, 2, UNIT, PATCHES)
    keep = jnp.where(first, turned[:, 0], turned[:, 1])
    give = jnp.where(first, turned[:, 1], turned[:, 0])
    got = to_sibling(give, pairs_z)
    block = jnp.concatenate([jnp.where(first, keep, got), jnp.where(first, got, keep)], axis=2)
    block = block.reshape(2 * UNIT, 2 * PATCHES)
    pieces, features = gather(unit, other, block, first, pairs_z)

    offsets = jnp.array([o for piece in piece_offsets() for o in piece], jnp.int32)
    source = (z + jnp.where(first, offsets, -offsets)) % pairs_z
    from_x, from_y = (at_x - source // 2 // SIDE) % SIDE, (at_y - source // 2 % SIDE) % SIDE
    inner = jnp.where(first, from_x, from_y)
    outer = jnp.where(first, from_y, from_x)
    starts = (inner * 2 + source % 2) * UNIT

    total = jax.ShapeDtypeStruct((2 * PATCHES, heads), f32)
    summed, stats = call(
        first_kernel,
        "project_first",
        (total, jax.ShapeDtypeStruct((TAIL, heads), f32)),
        (starts, outer, *features, *pieces[:7]),
        2,
        [pltpu.VMEM((FULL, 2 * PATCHES), bf16)],
        2 * 512 * 2688 * heads,
        6 * 2**20,
    )
    partial = jax.ShapeDtypeStruct((PATCHES + 8, heads), f32)
    mine, send = call(
        last_kernel,
        "project_last",
        (partial, partial),
        (starts, outer, core.reshape(1), *features, *pieces[7:], summed, stats),
        3,
        [
            pltpu.VMEM((2 * HALF, 2 * PATCHES), bf16),
            pltpu.VMEM((2 * HALF, heads), bf16),
            pltpu.VMEM((2 * PATCHES, heads), f32),
        ],
        2 * 512 * 384 * heads,
        2 * 2**20,
    )
    received = to_sibling(send, pairs_z)

    group_row = jax.ShapeDtypeStruct((1, groups), f32)
    probs, old_weights = call(
        scores_kernel,
        "scores",
        (jax.ShapeDtypeStruct((heads // HD, PATCHES, PATCHES), f32), group_row),
        (queries, keys, group_weights.reshape(1, groups)),
        flops=2 * PATCHES * PATCHES * heads,
    )
    out = jax.ShapeDtypeStruct(queries.shape, bf16)
    query_grad, key_grad, value_grad, new_weights = call(
        attention_kernel,
        "attention",
        (out, out, out, group_row),
        (group_ids, mine, received, old_weights, probs, queries, keys, values),
        1,
        flops=8 * PATCHES * PATCHES * heads,
        moved=3 * 2**20,
    )
    return query_grad, key_grad, value_grad, new_weights.reshape(groups)


def solution(mesh):
    placed = (
        P("dp", "mp"),
        P("mp", "dp"),
        P("dp", "mp"),
        P("dp", "mp"),
        P("dp", "mp"),
        P("dp"),
        P("dp"),
        P(),
    )
    return jax.shard_map(
        functools.partial(per_device, mesh.shape["dp"] // 2),
        mesh=mesh,
        in_specs=placed,
        out_specs=(P("dp", "mp"), P("dp", "mp"), P("dp", "mp"), P()),
        check_vma=False,
    )
```

```python
import functools

import jax
import jax.numpy as jnp
from jax import lax
from jax.experimental import pallas as pl
from jax.experimental.pallas import tpu as pltpu
from jax.sharding import PartitionSpec as P

HD = 128
PATCHES = 256
ROBUST_RATE = 0.5
SIDE = 4
FAR = 8
UNIT = 96
STATS = 4
TAIL = 16
HALF = 2 * UNIT + TAIL
FULL = 4 * UNIT + TAIL
ALL = ("dp", "mp")


def along_z(x, step0, step1, pairs_z):
    pairs = [
        (2 * z + c, 2 * ((z + step) % pairs_z) + c)
        for z in range(pairs_z)
        for c, step in ((0, step0), (1, step1))
    ]
    return lax.ppermute(x, "dp", pairs)


def to_sibling(x, pairs_z):
    return lax.ppermute(x, "dp", [(i, i ^ 1) for i in range(2 * pairs_z)])


def exchange(x, flip, first_axis, pairs_z):
    pairs = []
    for d in range(2 * pairs_z):
        on_x = (d % 2 == 0) == first_axis
        for m in range(SIDE * SIDE):
            i, j = divmod(m, SIDE)
            to = (i ^ flip) * SIDE + j if on_x else i * SIDE + (j ^ flip)
            pairs.append((d * SIDE * SIDE + m, d * SIDE * SIDE + to))
    return lax.ppermute(x, ALL, pairs)


def gather(unit, block, pairs_z):
    tie = lax.optimization_barrier
    mine = along_z(unit, FAR, -FAR, pairs_z)
    opposite = along_z(unit, -FAR, FAR, pairs_z)
    mine, opposite = meet(3300000000, mine, opposite)
    mine, opposite, block = tie((mine, opposite, block))
    passed = exchange(block, 1, True, pairs_z)
    farthest = along_z(mine, FAR, -FAR, pairs_z)
    (farthest,) = meet(3300000000, farthest)
    farthest, passed = tie((farthest, passed))
    block = stack([block, passed])
    bundle = join_units(unit, opposite, farthest, mine)
    pieces = [bundle]
    p = q = bundle
    for step, cost in enumerate((3300000000, 8800000000, 22000000000)):
        p = along_z(p, 1, -1, pairs_z)
        q = along_z(q, -1, 1, pairs_z)
        passed = exchange(block, (3, 1, 3)[step], step == 0, pairs_z)
        p, q = meet(cost, p, q)
        if step < 2:
            p, q, passed = tie((p, q, passed))
            block = stack([block, passed])
        pieces += [p, q]
    half = passed
    p = along_z(p[:HALF], 1, -1, pairs_z)
    q = along_z(q[UNIT : UNIT + HALF], -1, 1, pairs_z)
    return pieces + [p, q], [block, half]


def piece_offsets():
    slots = [0, FAR, 2 * FAR, -FAR]
    offsets = [slots]
    for k in range(1, FAR // 2):
        offsets += [[o - k for o in slots], [o + k for o in slots]]
    k = FAR // 2
    offsets += [[o - k for o in slots[:2]], [o + k for o in slots[1:3]]]
    return offsets


def unit_kernel(group, loss, weight_ref, unit_ref):
    heads = weight_ref.shape[1]
    unit_ref[pl.ds(0, UNIT), :] = weight_ref[...]
    x = jnp.full((TAIL, heads), loss[0], jnp.float32)
    high = x.astype(jnp.bfloat16).astype(jnp.float32)
    middle = (x - high).astype(jnp.bfloat16).astype(jnp.float32)
    low = x - high - middle
    row = lax.broadcasted_iota(jnp.int32, x.shape, 0)
    lane = lax.broadcasted_iota(jnp.int32, x.shape, 1)
    value = jnp.where(row == 0, 1.0, jnp.where(row == 1, high, jnp.where(row == 2, middle, low)))
    value = jnp.where((row < STATS) & (lane == group[0]), value, 0.0)
    unit_ref[pl.ds(UNIT, TAIL), :] = value.astype(jnp.bfloat16)


def join_kernel(*refs):
    *units, out = refs
    tail = jnp.zeros((TAIL, out.shape[1]), jnp.float32)
    for i, ref in enumerate(units):
        out[pl.ds(row_of(i), UNIT), :] = ref[pl.ds(0, UNIT), :]
        rows = ref[pl.ds(UNIT, TAIL), :].astype(jnp.float32)
        tail += pltpu.roll(rows, STATS * i, 0) if i else rows
    out[pl.ds(2 * UNIT, TAIL), :] = tail.astype(jnp.bfloat16)


def row_of(i):
    return i * UNIT + (TAIL if i >= 2 else 0)


def copy_kernel(*refs):
    half = len(refs) // 2
    for given, out in zip(refs[:half], refs[half:]):
        out[...] = given[...]


def stack_kernel(*refs):
    *blocks, out = refs
    rows = blocks[0].shape[0]
    for i, ref in enumerate(blocks):
        out[pl.ds(i * rows, rows), :] = ref[...]


def scores_kernel(q_ref, k_ref, gw_ref, probs_ref, weights_ref):
    weights_ref[...] = gw_ref[...]
    factor = 1.0 / jnp.sqrt(jnp.float32(HD))
    for h in range(q_ref.shape[1] // HD):
        cols = slice(h * HD, (h + 1) * HD)
        scores = lax.dot_general(
            q_ref[:, cols],
            k_ref[:, cols],
            (((1,), (1,)), ((), ())),
            preferred_element_type=jnp.float32,
        )
        raised = jnp.exp(scores * factor)
        probs_ref[h] = raised / jnp.sum(raised, axis=1, keepdims=True)


def pick_rows(starts, outers, slot, blocks, xs_ref, at):
    row = pl.multiple_of(starts[slot], 32)
    for i, block in enumerate(blocks):

        @pl.when(outers[slot] == i)
        def _():
            xs_ref[pl.ds(at, UNIT), :] = block[pl.ds(row, UNIT), :]


def product_of(xs, weight):
    return lax.dot_general(
        xs, weight, (((0,), (0,)), ((), ())), preferred_element_type=jnp.float32
    )


def first_kernel(starts, outers, *refs):
    blocks, pieces, (acc_ref, stats_ref, xs_ref) = refs[:2], refs[2:-3], refs[-3:]
    xs_ref[pl.ds(2 * UNIT, TAIL), :] = jnp.zeros((TAIL, xs_ref.shape[1]), xs_ref.dtype)
    stats_ref[...] = jnp.zeros_like(stats_ref)
    for i, piece in enumerate(pieces):
        for k in range(4):
            pick_rows(starts, outers, 4 * i + k, blocks, xs_ref, row_of(k))
        product = product_of(xs_ref[...], piece[...])
        if i == 0:
            acc_ref[...] = product
        else:
            acc_ref[...] += product
        stats_ref[...] += piece[pl.ds(2 * UNIT, TAIL), :].astype(jnp.float32)


def last_kernel(starts, outers, core, *refs):
    blocks, (p_ref, q_ref, acc_ref, stats_ref, mine_ref, send_ref, xs_ref, w_ref, sum_ref) = refs[:2], refs[2:]
    for k, at in enumerate((0, UNIT, HALF, HALF + UNIT + TAIL)):
        pick_rows(starts, outers, 28 + k, blocks, xs_ref, at)
    for at in (2 * UNIT, HALF + UNIT):
        xs_ref[pl.ds(at, TAIL), :] = jnp.zeros((TAIL, xs_ref.shape[1]), xs_ref.dtype)
    w_ref[pl.ds(0, HALF), :] = p_ref[...]
    w_ref[pl.ds(HALF, HALF), :] = q_ref[...]
    sum_ref[...] = acc_ref[...] + product_of(xs_ref[...], w_ref[...])
    stats = stats_ref[...]
    row = lax.broadcasted_iota(jnp.int32, stats.shape, 0)
    stats += jnp.where(row < 8, p_ref[pl.ds(2 * UNIT, TAIL), :].astype(jnp.float32), 0.0)
    middle = (row >= 4) & (row < 12)
    stats += jnp.where(middle, q_ref[pl.ds(UNIT, TAIL), :].astype(jnp.float32), 0.0)
    count = jnp.sum(jnp.where(row % 4 == 0, stats, 0.0), axis=0, keepdims=True)
    total = jnp.sum(jnp.where(row % 4 == 0, 0.0, stats), axis=0, keepdims=True)
    row8 = row[:8]
    tail = jnp.where(row8 == 0, count, jnp.where(row8 == 1, total, 0.0))
    here = pl.multiple_of(core[0] * PATCHES, PATCHES)
    there = pl.multiple_of((1 - core[0]) * PATCHES, PATCHES)
    mine_ref[pl.ds(0, PATCHES), :] = sum_ref[pl.ds(here, PATCHES), :]
    send_ref[pl.ds(0, PATCHES), :] = sum_ref[pl.ds(there, PATCHES), :]
    mine_ref[pl.ds(PATCHES, 8), :] = tail
    send_ref[pl.ds(PATCHES, 8), :] = tail


def attention_kernel(group, mine_ref, got_ref, gw_ref, probs_ref, q_ref, k_ref, v_ref, dq_ref, dk_ref, dv_ref, nw_ref):
    f32, bf16 = jnp.float32, jnp.bfloat16
    width = gw_ref.shape[1]
    tail = mine_ref[pl.ds(PATCHES, 8), :] + got_ref[pl.ds(PATCHES, 8), :]
    counts, totals = tail[0:1, :width], tail[1:2, :width]
    floored = jnp.maximum(counts, 1.0)
    raised = gw_ref[...] * jnp.exp(ROBUST_RATE * (totals / floored))
    new_weights = raised / jnp.sum(raised, axis=1, keepdims=True)
    nw_ref[...] = new_weights
    label = lax.broadcasted_iota(jnp.int32, (1, width), 1)
    scale = jnp.sum(
        jnp.where(label == group[0], new_weights / floored, 0.0), axis=1, keepdims=True
    )
    product = mine_ref[pl.ds(0, PATCHES), :] + got_ref[pl.ds(0, PATCHES), :]
    head_grad = (product * scale).astype(bf16)
    factor = 1.0 / jnp.sqrt(f32(HD))
    rows_by_rows = (((1,), (1,)), ((), ()))
    columns = (((0,), (0,)), ((), ()))
    plain = (((1,), (0,)), ((), ()))
    dot = functools.partial(lax.dot_general, preferred_element_type=f32)
    for h in range(q_ref.shape[1] // HD):
        cols = slice(h * HD, (h + 1) * HD)
        q, k, v, g = q_ref[:, cols], k_ref[:, cols], v_ref[:, cols], head_grad[:, cols]
        probs = probs_ref[h]
        dv_ref[:, cols] = dot(probs.astype(bf16), g, columns).astype(bf16)
        prob_grad = dot(g, v, rows_by_rows)
        centre = jnp.sum(probs * prob_grad, axis=1, keepdims=True)
        score = (probs * (prob_grad - centre)).astype(bf16)
        dq_ref[:, cols] = (dot(score, k, plain) * factor).astype(bf16)
        dk_ref[:, cols] = (dot(score, q, columns) * factor).astype(bf16)


VM = pl.BlockSpec(memory_space=pltpu.VMEM)
SM = pl.BlockSpec(memory_space=pltpu.SMEM)


def call(kernel, name, out_shape, operands, scalars=0, scratch=(), flops=0, moved=2**20):
    outs = jax.tree.map(lambda _: VM, out_shape)
    return pl.pallas_call(
        kernel,
        out_shape=out_shape,
        in_specs=[SM] * scalars + [VM] * (len(operands) - scalars),
        out_specs=outs,
        scratch_shapes=scratch,
        compiler_params=pltpu.CompilerParams(vmem_limit_bytes=16 * 2**20),
        cost_estimate=pl.CostEstimate(flops=flops, bytes_accessed=moved, transcendentals=0),
        name=name,
    )(*operands)


def join_units(*units):
    shape = jax.ShapeDtypeStruct((FULL, units[0].shape[1]), units[0].dtype)
    return call(join_kernel, "join_units", shape, units)


def meet(flops, *arrays):
    shapes = tuple(jax.ShapeDtypeStruct(a.shape, a.dtype) for a in arrays)
    return call(copy_kernel, "meet", shapes, arrays, flops=flops)


def stack(blocks):
    rows, width = blocks[0].shape
    shape = jax.ShapeDtypeStruct((len(blocks) * rows, width), blocks[0].dtype)
    return call(stack_kernel, "stack", shape, blocks)


def per_device(pairs_z, cotangent, out_weight, queries, keys, values, image_loss, group_ids, group_weights):
    f32, bf16 = jnp.float32, jnp.bfloat16
    groups = group_weights.shape[0]
    heads = queries.shape[1]
    core = lax.axis_index("dp") % 2
    first = core == 0
    z = lax.axis_index("dp") // 2
    mp = lax.axis_index("mp")
    at_x, at_y = mp // SIDE, mp % SIDE

    unit = call(
        unit_kernel,
        "make_unit",
        jax.ShapeDtypeStruct((UNIT + TAIL, heads), bf16),
        (group_ids, image_loss, out_weight.T),
        2,
        moved=2**17,
    )

    turned = cotangent.T.reshape(2, 2, UNIT, PATCHES)
    keep = jnp.where(first, turned[:, 0], turned[:, 1])
    give = jnp.where(first, turned[:, 1], turned[:, 0])
    got = to_sibling(give, pairs_z)
    block = jnp.concatenate([jnp.where(first, keep, got), jnp.where(first, got, keep)], axis=2)
    block = block.reshape(2 * UNIT, 2 * PATCHES)
    pieces, features = gather(unit, block, pairs_z)

    offsets = jnp.array([o for piece in piece_offsets() for o in piece], jnp.int32)
    source = (z + jnp.where(first, offsets, -offsets)) % pairs_z
    from_x, from_y = at_x ^ (source // 2 // SIDE), at_y ^ (source // 2 % SIDE)
    inner = jnp.where(first, from_x, from_y)
    outer = jnp.where(first, from_y, from_x)
    inner, outer = inner ^ (inner >> 1), outer ^ (outer >> 1)
    starts = ((outer % 2 * SIDE + inner) * 2 + source % 2) * UNIT
    outer = outer // 2

    total = jax.ShapeDtypeStruct((2 * PATCHES, heads), f32)
    summed, stats = call(
        first_kernel,
        "project_first",
        (total, jax.ShapeDtypeStruct((TAIL, heads), f32)),
        (starts, outer, *features, *pieces[:7]),
        2,
        [pltpu.VMEM((FULL, 2 * PATCHES), bf16)],
        2 * 512 * 2688 * heads,
        6 * 2**20,
    )
    partial = jax.ShapeDtypeStruct((PATCHES + 8, heads), f32)
    mine, send = call(
        last_kernel,
        "project_last",
        (partial, partial),
        (starts, outer, core.reshape(1), *features, *pieces[7:], summed, stats),
        3,
        [
            pltpu.VMEM((2 * HALF, 2 * PATCHES), bf16),
            pltpu.VMEM((2 * HALF, heads), bf16),
            pltpu.VMEM((2 * PATCHES, heads), f32),
        ],
        2 * 512 * 384 * heads,
        2 * 2**20,
    )
    received = to_sibling(send, pairs_z)

    group_row = jax.ShapeDtypeStruct((1, groups), f32)
    probs, old_weights = call(
        scores_kernel,
        "scores",
        (jax.ShapeDtypeStruct((heads // HD, PATCHES, PATCHES), f32), group_row),
        (queries, keys, group_weights.reshape(1, groups)),
        flops=2 * PATCHES * PATCHES * heads,
    )
    out = jax.ShapeDtypeStruct(queries.shape, bf16)
    query_grad, key_grad, value_grad, new_weights = call(
        attention_kernel,
        "attention",
        (out, out, out, group_row),
        (group_ids, mine, received, old_weights, probs, queries, keys, values),
        1,
        flops=8 * PATCHES * PATCHES * heads,
        moved=3 * 2**20,
    )
    return query_grad, key_grad, value_grad, new_weights.reshape(groups)


def solution(mesh):
    placed = (
        P("dp", "mp"),
        P("mp", "dp"),
        P("dp", "mp"),
        P("dp", "mp"),
        P("dp", "mp"),
        P("dp"),
        P("dp"),
        P(),
    )
    return jax.shard_map(
        functools.partial(per_device, mesh.shape["dp"] // 2),
        mesh=mesh,
        in_specs=placed,
        out_specs=(P("dp", "mp"), P("dp", "mp"), P("dp", "mp"), P()),
        check_vma=False,
    )
```

```python
import functools

import jax
import jax.numpy as jnp
from jax import lax
from jax.experimental import pallas as pl
from jax.experimental.pallas import tpu as pltpu
from jax.sharding import PartitionSpec as P

HD = 128
PATCHES = 256
ROBUST_RATE = 0.5
SIDE = 4
FAR = 8
UNIT = 96
STATS = 4
TAIL = 16
HALF = 2 * UNIT + TAIL
FULL = 4 * UNIT + TAIL
ALL = ("dp", "mp")


def along_z(x, step0, step1, pairs_z):
    pairs = [
        (2 * z + c, 2 * ((z + step) % pairs_z) + c)
        for z in range(pairs_z)
        for c, step in ((0, step0), (1, step1))
    ]
    return lax.ppermute(x, "dp", pairs)


def to_sibling(x, pairs_z):
    return lax.ppermute(x, "dp", [(i, i ^ 1) for i in range(2 * pairs_z)])


def exchange(x, flip, first_axis, pairs_z):
    pairs = []
    for d in range(2 * pairs_z):
        on_x = (d % 2 == 0) == first_axis
        for m in range(SIDE * SIDE):
            i, j = divmod(m, SIDE)
            to = (i ^ flip) * SIDE + j if on_x else i * SIDE + (j ^ flip)
            pairs.append((d * SIDE * SIDE + m, d * SIDE * SIDE + to))
    return lax.ppermute(x, ALL, pairs)


def gather(unit, block, pairs_z):
    tie = lax.optimization_barrier
    mine = along_z(unit, FAR, -FAR, pairs_z)
    opposite = along_z(unit, -FAR, FAR, pairs_z)
    passed = exchange(block, 1, True, pairs_z)
    mine, opposite = meet(2, mine, opposite)
    farthest = along_z(mine, FAR, -FAR, pairs_z)
    block = stack([block, passed])
    passed = exchange(block, 3, True, pairs_z)
    (farthest,) = meet(4, farthest)
    farthest, passed, block = tie((farthest, passed, block))
    block = stack([block, passed])
    bundle = join_units(unit, opposite, farthest, mine)
    pieces = [bundle]
    p = q = bundle
    for step, wait in enumerate((6, 6, 8)):
        p = along_z(p, 1, -1, pairs_z)
        q = along_z(q, -1, 1, pairs_z)
        if step < 2:
            passed = exchange(block, 1 + 2 * step, False, pairs_z)
        p, q = meet(wait, p, q)
        if step == 0:
            block = stack([block, passed])
        pieces += [p, q]
    half = passed
    p = along_z(p[:HALF], 1, -1, pairs_z)
    q = along_z(q[UNIT : UNIT + HALF], -1, 1, pairs_z)
    return pieces + [p, q], [block, half]


def piece_offsets():
    slots = [0, FAR, 2 * FAR, -FAR]
    offsets = [slots]
    for k in range(1, FAR // 2):
        offsets += [[o - k for o in slots], [o + k for o in slots]]
    k = FAR // 2
    offsets += [[o - k for o in slots[:2]], [o + k for o in slots[1:3]]]
    return offsets


def unit_kernel(group, loss, weight_ref, unit_ref):
    heads = weight_ref.shape[1]
    unit_ref[pl.ds(0, UNIT), :] = weight_ref[...]
    x = jnp.full((TAIL, heads), loss[0], jnp.float32)
    high = x.astype(jnp.bfloat16).astype(jnp.float32)
    middle = (x - high).astype(jnp.bfloat16).astype(jnp.float32)
    low = x - high - middle
    row = lax.broadcasted_iota(jnp.int32, x.shape, 0)
    lane = lax.broadcasted_iota(jnp.int32, x.shape, 1)
    value = jnp.where(row == 0, 1.0, jnp.where(row == 1, high, jnp.where(row == 2, middle, low)))
    value = jnp.where((row < STATS) & (lane == group[0]), value, 0.0)
    unit_ref[pl.ds(UNIT, TAIL), :] = value.astype(jnp.bfloat16)


def join_kernel(*refs):
    *units, out = refs
    tail = jnp.zeros((TAIL, out.shape[1]), jnp.float32)
    for i, ref in enumerate(units):
        out[pl.ds(row_of(i), UNIT), :] = ref[pl.ds(0, UNIT), :]
        rows = ref[pl.ds(UNIT, TAIL), :].astype(jnp.float32)
        tail += pltpu.roll(rows, STATS * i, 0) if i else rows
    out[pl.ds(2 * UNIT, TAIL), :] = tail.astype(jnp.bfloat16)


def row_of(i):
    return i * UNIT + (TAIL if i >= 2 else 0)


def copy_kernel(*refs):
    half = len(refs) // 2
    for given, out in zip(refs[:half], refs[half:]):
        out[...] = given[...]


def stack_kernel(*refs):
    *blocks, out = refs
    rows = blocks[0].shape[0]
    for i, ref in enumerate(blocks):
        out[pl.ds(i * rows, rows), :] = ref[...]


def scores_kernel(q_ref, k_ref, gw_ref, probs_ref, weights_ref):
    weights_ref[...] = gw_ref[...]
    factor = 1.0 / jnp.sqrt(jnp.float32(HD))
    for h in range(q_ref.shape[1] // HD):
        cols = slice(h * HD, (h + 1) * HD)
        scores = lax.dot_general(
            q_ref[:, cols],
            k_ref[:, cols],
            (((1,), (1,)), ((), ())),
            preferred_element_type=jnp.float32,
        )
        raised = jnp.exp(scores * factor)
        probs_ref[h] = raised / jnp.sum(raised, axis=1, keepdims=True)


def pick_rows(starts, outers, slot, blocks, xs_ref, at):
    row = pl.multiple_of(starts[slot], 32)
    for i, block in enumerate(blocks):

        @pl.when(outers[slot] == i)
        def _():
            xs_ref[pl.ds(at, UNIT), :] = block[pl.ds(row, UNIT), :]


def product_of(xs, weight):
    return lax.dot_general(
        xs, weight, (((0,), (0,)), ((), ())), preferred_element_type=jnp.float32
    )


def first_kernel(starts, outers, *refs):
    blocks, pieces, (acc_ref, stats_ref, xs_ref) = refs[:2], refs[2:-3], refs[-3:]
    xs_ref[pl.ds(2 * UNIT, TAIL), :] = jnp.zeros((TAIL, xs_ref.shape[1]), xs_ref.dtype)
    stats_ref[...] = jnp.zeros_like(stats_ref)
    for i, piece in enumerate(pieces):
        for k in range(4):
            pick_rows(starts, outers, 4 * i + k, blocks, xs_ref, row_of(k))
        product = product_of(xs_ref[...], piece[...])
        if i == 0:
            acc_ref[...] = product
        else:
            acc_ref[...] += product
        stats_ref[...] += piece[pl.ds(2 * UNIT, TAIL), :].astype(jnp.float32)


def last_kernel(starts, outers, core, *refs):
    blocks, (p_ref, q_ref, acc_ref, stats_ref, mine_ref, send_ref, xs_ref, w_ref, sum_ref) = refs[:2], refs[2:]
    for k, at in enumerate((0, UNIT, HALF, HALF + UNIT + TAIL)):
        pick_rows(starts, outers, 28 + k, blocks, xs_ref, at)
    for at in (2 * UNIT, HALF + UNIT):
        xs_ref[pl.ds(at, TAIL), :] = jnp.zeros((TAIL, xs_ref.shape[1]), xs_ref.dtype)
    w_ref[pl.ds(0, HALF), :] = p_ref[...]
    w_ref[pl.ds(HALF, HALF), :] = q_ref[...]
    sum_ref[...] = acc_ref[...] + product_of(xs_ref[...], w_ref[...])
    stats = stats_ref[...]
    row = lax.broadcasted_iota(jnp.int32, stats.shape, 0)
    stats += jnp.where(row < 8, p_ref[pl.ds(2 * UNIT, TAIL), :].astype(jnp.float32), 0.0)
    middle = (row >= 4) & (row < 12)
    stats += jnp.where(middle, q_ref[pl.ds(UNIT, TAIL), :].astype(jnp.float32), 0.0)
    count = jnp.sum(jnp.where(row % 4 == 0, stats, 0.0), axis=0, keepdims=True)
    total = jnp.sum(jnp.where(row % 4 == 0, 0.0, stats), axis=0, keepdims=True)
    row8 = row[:8]
    tail = jnp.where(row8 == 0, count, jnp.where(row8 == 1, total, 0.0))
    here = pl.multiple_of(core[0] * PATCHES, PATCHES)
    there = pl.multiple_of((1 - core[0]) * PATCHES, PATCHES)
    mine_ref[pl.ds(0, PATCHES), :] = sum_ref[pl.ds(here, PATCHES), :]
    send_ref[pl.ds(0, PATCHES), :] = sum_ref[pl.ds(there, PATCHES), :]
    mine_ref[pl.ds(PATCHES, 8), :] = tail
    send_ref[pl.ds(PATCHES, 8), :] = tail


def attention_kernel(group, mine_ref, got_ref, gw_ref, probs_ref, q_ref, k_ref, v_ref, dq_ref, dk_ref, dv_ref, nw_ref):
    f32, bf16 = jnp.float32, jnp.bfloat16
    width = gw_ref.shape[1]
    tail = mine_ref[pl.ds(PATCHES, 8), :] + got_ref[pl.ds(PATCHES, 8), :]
    counts, totals = tail[0:1, :width], tail[1:2, :width]
    floored = jnp.maximum(counts, 1.0)
    raised = gw_ref[...] * jnp.exp(ROBUST_RATE * (totals / floored))
    new_weights = raised / jnp.sum(raised, axis=1, keepdims=True)
    nw_ref[...] = new_weights
    label = lax.broadcasted_iota(jnp.int32, (1, width), 1)
    scale = jnp.sum(
        jnp.where(label == group[0], new_weights / floored, 0.0), axis=1, keepdims=True
    )
    product = mine_ref[pl.ds(0, PATCHES), :] + got_ref[pl.ds(0, PATCHES), :]
    head_grad = (product * scale).astype(bf16)
    factor = 1.0 / jnp.sqrt(f32(HD))
    rows_by_rows = (((1,), (1,)), ((), ()))
    columns = (((0,), (0,)), ((), ()))
    plain = (((1,), (0,)), ((), ()))
    dot = functools.partial(lax.dot_general, preferred_element_type=f32)
    for h in range(q_ref.shape[1] // HD):
        cols = slice(h * HD, (h + 1) * HD)
        q, k, v, g = q_ref[:, cols], k_ref[:, cols], v_ref[:, cols], head_grad[:, cols]
        probs = probs_ref[h]
        dv_ref[:, cols] = dot(probs.astype(bf16), g, columns).astype(bf16)
        prob_grad = dot(g, v, rows_by_rows)
        centre = jnp.sum(probs * prob_grad, axis=1, keepdims=True)
        score = (probs * (prob_grad - centre)).astype(bf16)
        dq_ref[:, cols] = (dot(score, k, plain) * factor).astype(bf16)
        dk_ref[:, cols] = (dot(score, q, columns) * factor).astype(bf16)


VM = pl.BlockSpec(memory_space=pltpu.VMEM)
SM = pl.BlockSpec(memory_space=pltpu.SMEM)


def call(kernel, name, out_shape, operands, scalars=0, scratch=(), flops=0, moved=2**20):
    outs = jax.tree.map(lambda _: VM, out_shape)
    return pl.pallas_call(
        kernel,
        out_shape=out_shape,
        in_specs=[SM] * scalars + [VM] * (len(operands) - scalars),
        out_specs=outs,
        scratch_shapes=scratch,
        compiler_params=pltpu.CompilerParams(vmem_limit_bytes=16 * 2**20),
        cost_estimate=pl.CostEstimate(flops=flops, bytes_accessed=moved, transcendentals=0),
        name=name,
    )(*operands)


def join_units(*units):
    shape = jax.ShapeDtypeStruct((FULL, units[0].shape[1]), units[0].dtype)
    return call(join_kernel, "join_units", shape, units)


def meet(microseconds, *arrays):
    places = [pl.BlockSpec(memory_space=pl.ANY)] * len(arrays)
    return pl.pallas_call(
        lambda *refs: None,
        out_shape=tuple(jax.ShapeDtypeStruct(a.shape, a.dtype) for a in arrays),
        in_specs=places,
        out_specs=tuple(places),
        input_output_aliases={i: i for i in range(len(arrays))},
        compiler_params=pltpu.CompilerParams(vmem_limit_bytes=2**20),
        cost_estimate=pl.CostEstimate(
            flops=microseconds * 10**9, bytes_accessed=0, transcendentals=0
        ),
        name="meet",
    )(*arrays)


def stack(blocks):
    rows, width = blocks[0].shape
    shape = jax.ShapeDtypeStruct((len(blocks) * rows, width), blocks[0].dtype)
    return call(stack_kernel, "stack", shape, blocks)


def per_device(pairs_z, cotangent, out_weight, queries, keys, values, image_loss, group_ids, group_weights):
    f32, bf16 = jnp.float32, jnp.bfloat16
    groups = group_weights.shape[0]
    heads = queries.shape[1]
    core = lax.axis_index("dp") % 2
    first = core == 0
    z = lax.axis_index("dp") // 2
    mp = lax.axis_index("mp")
    at_x, at_y = mp // SIDE, mp % SIDE

    unit = call(
        unit_kernel,
        "make_unit",
        jax.ShapeDtypeStruct((UNIT + TAIL, heads), bf16),
        (group_ids, image_loss, out_weight.T),
        2,
        moved=2**17,
    )

    turned = cotangent.T.reshape(2, 2, UNIT, PATCHES)
    keep = jnp.where(first, turned[:, 0], turned[:, 1])
    give = jnp.where(first, turned[:, 1], turned[:, 0])
    got = to_sibling(give, pairs_z)
    block = jnp.concatenate([jnp.where(first, keep, got), jnp.where(first, got, keep)], axis=2)
    block = block.reshape(2 * UNIT, 2 * PATCHES)
    pieces, features = gather(unit, block, pairs_z)

    offsets = jnp.array([o for piece in piece_offsets() for o in piece], jnp.int32)
    source = (z + jnp.where(first, offsets, -offsets)) % pairs_z
    from_x, from_y = at_x ^ (source // 2 // SIDE), at_y ^ (source // 2 % SIDE)
    inner = jnp.where(first, from_x, from_y)
    outer = jnp.where(first, from_y, from_x)
    inner, outer = inner ^ (inner >> 1), outer ^ (outer >> 1)
    starts = ((outer % 2 * SIDE + inner) * 2 + source % 2) * UNIT
    outer = outer // 2

    total = jax.ShapeDtypeStruct((2 * PATCHES, heads), f32)
    summed, stats = call(
        first_kernel,
        "project_first",
        (total, jax.ShapeDtypeStruct((TAIL, heads), f32)),
        (starts, outer, *features, *pieces[:7]),
        2,
        [pltpu.VMEM((FULL, 2 * PATCHES), bf16)],
        2 * 512 * 2688 * heads,
        6 * 2**20,
    )
    partial = jax.ShapeDtypeStruct((PATCHES + 8, heads), f32)
    mine, send = call(
        last_kernel,
        "project_last",
        (partial, partial),
        (starts, outer, core.reshape(1), *features, *pieces[7:], summed, stats),
        3,
        [
            pltpu.VMEM((2 * HALF, 2 * PATCHES), bf16),
            pltpu.VMEM((2 * HALF, heads), bf16),
            pltpu.VMEM((2 * PATCHES, heads), f32),
        ],
        2 * 512 * 384 * heads,
        2 * 2**20,
    )
    received = to_sibling(send, pairs_z)

    group_row = jax.ShapeDtypeStruct((1, groups), f32)
    probs, old_weights = call(
        scores_kernel,
        "scores",
        (jax.ShapeDtypeStruct((heads // HD, PATCHES, PATCHES), f32), group_row),
        (queries, keys, group_weights.reshape(1, groups)),
        flops=2 * PATCHES * PATCHES * heads,
    )
    out = jax.ShapeDtypeStruct(queries.shape, bf16)
    query_grad, key_grad, value_grad, new_weights = call(
        attention_kernel,
        "attention",
        (out, out, out, group_row),
        (group_ids, mine, received, old_weights, probs, queries, keys, values),
        1,
        flops=8 * PATCHES * PATCHES * heads,
        moved=3 * 2**20,
    )
    return query_grad, key_grad, value_grad, new_weights.reshape(groups)


def solution(mesh):
    placed = (
        P("dp", "mp"),
        P("mp", "dp"),
        P("dp", "mp"),
        P("dp", "mp"),
        P("dp", "mp"),
        P("dp"),
        P("dp"),
        P(),
    )
    return jax.shard_map(
        functools.partial(per_device, mesh.shape["dp"] // 2),
        mesh=mesh,
        in_specs=placed,
        out_specs=(P("dp", "mp"), P("dp", "mp"), P("dp", "mp"), P()),
        check_vma=False,
    )
```

```python
import functools

import jax
import jax.numpy as jnp
from jax import lax
from jax.experimental import pallas as pl
from jax.experimental.pallas import tpu as pltpu
from jax.sharding import PartitionSpec as P

HD = 128
PATCHES = 256
ROBUST_RATE = 0.5
SIDE = 4
FAR = 11
STEPS = 5
UNIT = 96
STATS = 4
TAIL = 16
HALF = 2 * UNIT + TAIL
FULL = 3 * UNIT + TAIL
ALL = ("dp", "mp")


def along_z(x, step0, step1, pairs_z):
    pairs = [
        (2 * z + c, 2 * ((z + step) % pairs_z) + c)
        for z in range(pairs_z)
        for c, step in ((0, step0), (1, step1))
    ]
    return lax.ppermute(x, "dp", pairs)


def to_sibling(x, pairs_z):
    return lax.ppermute(x, "dp", [(i, i ^ 1) for i in range(2 * pairs_z)])


def exchange(x, flip, first_axis, pairs_z):
    pairs = []
    for d in range(2 * pairs_z):
        on_x = (d % 2 == 0) == first_axis
        for m in range(SIDE * SIDE):
            i, j = divmod(m, SIDE)
            to = (i ^ flip) * SIDE + j if on_x else i * SIDE + (j ^ flip)
            pairs.append((d * SIDE * SIDE + m, d * SIDE * SIDE + to))
    return lax.ppermute(x, ALL, pairs)


def gather(unit, block, pairs_z):
    tie = lax.optimization_barrier
    behind = along_z(unit, FAR, -FAR, pairs_z)
    ahead = along_z(unit, -FAR, FAR, pairs_z)
    passed = exchange(block, 1, True, pairs_z)
    behind, ahead = meet(2, behind, ahead)
    behind, ahead, block, passed = tie((behind, ahead, block, passed))
    bundle = join_units(unit, ahead, behind)
    block, bundle = tie((stack([block, passed]), bundle))
    pieces = [bundle]
    p = q = bundle
    for step, wait in enumerate((2, 7, 5, 5)):
        p = along_z(p, 1, -1, pairs_z)
        q = along_z(q, -1, 1, pairs_z)
        if step < 3:
            passed = exchange(block, (3, 1, 3)[step], step == 0, pairs_z)
        if step < 2:
            block = stack([block, passed])
        p, q = meet(wait, p, q)
        pieces += [p, q]
    p = along_z(p[:HALF], 1, -1, pairs_z)
    q = along_z(q, -1, 1, pairs_z)
    return pieces + [p, q], [block, passed]


def piece_offsets():
    units = [0, FAR, -FAR]
    offsets = [units]
    for k in range(1, STEPS + 1):
        offsets += [[o - k for o in units], [o + k for o in units]]
    offsets[-2] = offsets[-2][:2]
    return offsets


def unit_kernel(group, loss, weight_ref, unit_ref):
    heads = weight_ref.shape[1]
    unit_ref[pl.ds(0, UNIT), :] = weight_ref[...]
    x = jnp.full((TAIL, heads), loss[0], jnp.float32)
    high = x.astype(jnp.bfloat16).astype(jnp.float32)
    middle = (x - high).astype(jnp.bfloat16).astype(jnp.float32)
    low = x - high - middle
    row = lax.broadcasted_iota(jnp.int32, x.shape, 0)
    lane = lax.broadcasted_iota(jnp.int32, x.shape, 1)
    value = jnp.where(row == 0, 1.0, jnp.where(row == 1, high, jnp.where(row == 2, middle, low)))
    value = jnp.where((row < STATS) & (lane == group[0]), value, 0.0)
    unit_ref[pl.ds(UNIT, TAIL), :] = value.astype(jnp.bfloat16)


def join_kernel(*refs):
    *units, out = refs
    tail = jnp.zeros((TAIL, out.shape[1]), jnp.float32)
    for i, ref in enumerate(units):
        out[pl.ds(row_of(i), UNIT), :] = ref[pl.ds(0, UNIT), :]
        rows = ref[pl.ds(UNIT, TAIL), :].astype(jnp.float32)
        tail += pltpu.roll(rows, STATS * i, 0) if i else rows
    out[pl.ds(2 * UNIT, TAIL), :] = tail.astype(jnp.bfloat16)


def row_of(i):
    return i * UNIT + (TAIL if i >= 2 else 0)


def copy_kernel(*refs):
    half = len(refs) // 2
    for given, out in zip(refs[:half], refs[half:]):
        out[...] = given[...]


def stack_kernel(*refs):
    *blocks, out = refs
    rows = blocks[0].shape[0]
    for i, ref in enumerate(blocks):
        out[pl.ds(i * rows, rows), :] = ref[...]


def scores_kernel(q_ref, k_ref, gw_ref, probs_ref, weights_ref):
    weights_ref[...] = gw_ref[...]
    factor = 1.0 / jnp.sqrt(jnp.float32(HD))
    for h in range(q_ref.shape[1] // HD):
        cols = slice(h * HD, (h + 1) * HD)
        scores = lax.dot_general(
            q_ref[:, cols],
            k_ref[:, cols],
            (((1,), (1,)), ((), ())),
            preferred_element_type=jnp.float32,
        )
        raised = jnp.exp(scores * factor)
        probs_ref[h] = raised / jnp.sum(raised, axis=1, keepdims=True)


def pick_rows(starts, outers, slot, blocks, xs_ref, at):
    row = pl.multiple_of(starts[slot], 32)
    for i, block in enumerate(blocks):

        @pl.when(outers[slot] == i)
        def _():
            xs_ref[pl.ds(at, UNIT), :] = block[pl.ds(row, UNIT), :]


def product_of(xs, weight):
    return lax.dot_general(
        xs, weight, (((0,), (0,)), ((), ())), preferred_element_type=jnp.float32
    )


def first_kernel(starts, outers, *refs):
    blocks, pieces, (acc_ref, stats_ref, xs_ref) = refs[:2], refs[2:-3], refs[-3:]
    xs_ref[pl.ds(2 * UNIT, TAIL), :] = jnp.zeros((TAIL, xs_ref.shape[1]), xs_ref.dtype)
    stats_ref[...] = jnp.zeros_like(stats_ref)
    for i, piece in enumerate(pieces):
        for k in range(3):
            pick_rows(starts, outers, 3 * i + k, blocks, xs_ref, row_of(k))
        product = product_of(xs_ref[...], piece[...])
        if i == 0:
            acc_ref[...] = product
        else:
            acc_ref[...] += product
        stats_ref[...] += piece[pl.ds(2 * UNIT, TAIL), :].astype(jnp.float32)


def last_kernel(starts, outers, core, *refs):
    blocks, (p_ref, q_ref, acc_ref, stats_ref, mine_ref, send_ref, xs_ref, w_ref, sum_ref) = refs[:2], refs[2:]
    for k, at in enumerate((0, UNIT, HALF, HALF + UNIT, 2 * HALF)):
        pick_rows(starts, outers, 27 + k, blocks, xs_ref, at)
    for at in (2 * UNIT, HALF + 2 * UNIT):
        xs_ref[pl.ds(at, TAIL), :] = jnp.zeros((TAIL, xs_ref.shape[1]), xs_ref.dtype)
    w_ref[pl.ds(0, HALF), :] = p_ref[...]
    w_ref[pl.ds(HALF, FULL), :] = q_ref[...]
    sum_ref[...] = acc_ref[...] + product_of(xs_ref[...], w_ref[...])
    stats = stats_ref[...]
    row = lax.broadcasted_iota(jnp.int32, stats.shape, 0)
    p_stats = p_ref[pl.ds(2 * UNIT, TAIL), :].astype(jnp.float32)
    stats += jnp.where(row < 2 * STATS, p_stats, 0.0)
    stats += q_ref[pl.ds(2 * UNIT, TAIL), :].astype(jnp.float32)
    count = jnp.sum(jnp.where(row % 4 == 0, stats, 0.0), axis=0, keepdims=True)
    total = jnp.sum(jnp.where(row % 4 == 0, 0.0, stats), axis=0, keepdims=True)
    row8 = row[:8]
    tail = jnp.where(row8 == 0, count, jnp.where(row8 == 1, total, 0.0))
    here = pl.multiple_of(core[0] * PATCHES, PATCHES)
    there = pl.multiple_of((1 - core[0]) * PATCHES, PATCHES)
    mine_ref[pl.ds(0, PATCHES), :] = sum_ref[pl.ds(here, PATCHES), :]
    send_ref[pl.ds(0, PATCHES), :] = sum_ref[pl.ds(there, PATCHES), :]
    mine_ref[pl.ds(PATCHES, 8), :] = tail
    send_ref[pl.ds(PATCHES, 8), :] = tail


def attention_kernel(group, mine_ref, got_ref, gw_ref, probs_ref, q_ref, k_ref, v_ref, dq_ref, dk_ref, dv_ref, nw_ref):
    f32, bf16 = jnp.float32, jnp.bfloat16
    width = gw_ref.shape[1]
    tail = mine_ref[pl.ds(PATCHES, 8), :] + got_ref[pl.ds(PATCHES, 8), :]
    counts, totals = tail[0:1, :width], tail[1:2, :width]
    floored = jnp.maximum(counts, 1.0)
    raised = gw_ref[...] * jnp.exp(ROBUST_RATE * (totals / floored))
    new_weights = raised / jnp.sum(raised, axis=1, keepdims=True)
    nw_ref[...] = new_weights
    label = lax.broadcasted_iota(jnp.int32, (1, width), 1)
    scale = jnp.sum(
        jnp.where(label == group[0], new_weights / floored, 0.0), axis=1, keepdims=True
    )
    product = mine_ref[pl.ds(0, PATCHES), :] + got_ref[pl.ds(0, PATCHES), :]
    head_grad = (product * scale).astype(bf16)
    factor = 1.0 / jnp.sqrt(f32(HD))
    rows_by_rows = (((1,), (1,)), ((), ()))
    columns = (((0,), (0,)), ((), ()))
    plain = (((1,), (0,)), ((), ()))
    dot = functools.partial(lax.dot_general, preferred_element_type=f32)
    for h in range(q_ref.shape[1] // HD):
        cols = slice(h * HD, (h + 1) * HD)
        q, k, v, g = q_ref[:, cols], k_ref[:, cols], v_ref[:, cols], head_grad[:, cols]
        probs = probs_ref[h]
        dv_ref[:, cols] = dot(probs.astype(bf16), g, columns).astype(bf16)
        prob_grad = dot(g, v, rows_by_rows)
        centre = jnp.sum(probs * prob_grad, axis=1, keepdims=True)
        score = (probs * (prob_grad - centre)).astype(bf16)
        dq_ref[:, cols] = (dot(score, k, plain) * factor).astype(bf16)
        dk_ref[:, cols] = (dot(score, q, columns) * factor).astype(bf16)


VM = pl.BlockSpec(memory_space=pltpu.VMEM)
SM = pl.BlockSpec(memory_space=pltpu.SMEM)


def call(kernel, name, out_shape, operands, scalars=0, scratch=(), flops=0, moved=2**20):
    outs = jax.tree.map(lambda _: VM, out_shape)
    return pl.pallas_call(
        kernel,
        out_shape=out_shape,
        in_specs=[SM] * scalars + [VM] * (len(operands) - scalars),
        out_specs=outs,
        scratch_shapes=scratch,
        compiler_params=pltpu.CompilerParams(vmem_limit_bytes=16 * 2**20),
        cost_estimate=pl.CostEstimate(flops=flops, bytes_accessed=moved, transcendentals=0),
        name=name,
    )(*operands)


def join_units(*units):
    shape = jax.ShapeDtypeStruct((FULL, units[0].shape[1]), units[0].dtype)
    return call(join_kernel, "join_units", shape, units)


def meet(microseconds, *arrays):
    places = [pl.BlockSpec(memory_space=pl.ANY)] * len(arrays)
    return pl.pallas_call(
        lambda *refs: None,
        out_shape=tuple(jax.ShapeDtypeStruct(a.shape, a.dtype) for a in arrays),
        in_specs=places,
        out_specs=tuple(places),
        input_output_aliases={i: i for i in range(len(arrays))},
        compiler_params=pltpu.CompilerParams(vmem_limit_bytes=2**20),
        cost_estimate=pl.CostEstimate(
            flops=microseconds * 10**9, bytes_accessed=0, transcendentals=0
        ),
        name="meet",
    )(*arrays)


def stack(blocks):
    rows, width = blocks[0].shape
    shape = jax.ShapeDtypeStruct((len(blocks) * rows, width), blocks[0].dtype)
    return call(stack_kernel, "stack", shape, blocks)


def per_device(pairs_z, cotangent, out_weight, queries, keys, values, image_loss, group_ids, group_weights):
    f32, bf16 = jnp.float32, jnp.bfloat16
    groups = group_weights.shape[0]
    heads = queries.shape[1]
    core = lax.axis_index("dp") % 2
    first = core == 0
    z = lax.axis_index("dp") // 2
    mp = lax.axis_index("mp")
    at_x, at_y = mp // SIDE, mp % SIDE

    unit = call(
        unit_kernel,
        "make_unit",
        jax.ShapeDtypeStruct((UNIT + TAIL, heads), bf16),
        (group_ids, image_loss, out_weight.T),
        2,
        moved=2**17,
    )

    turned = cotangent.T.reshape(2, 2, UNIT, PATCHES)
    keep = jnp.where(first, turned[:, 0], turned[:, 1])
    give = jnp.where(first, turned[:, 1], turned[:, 0])
    got = to_sibling(give, pairs_z)
    block = jnp.concatenate([jnp.where(first, keep, got), jnp.where(first, got, keep)], axis=2)
    block = block.reshape(2 * UNIT, 2 * PATCHES)
    pieces, features = gather(unit, block, pairs_z)

    offsets = jnp.array([o for piece in piece_offsets() for o in piece], jnp.int32)
    source = (z + jnp.where(first, offsets, -offsets)) % pairs_z
    from_x, from_y = at_x ^ (source // 2 // SIDE), at_y ^ (source // 2 % SIDE)
    inner = jnp.where(first, from_x, from_y)
    outer = jnp.where(first, from_y, from_x)
    inner, outer = inner ^ (inner >> 1), outer ^ (outer >> 1)
    starts = ((outer % 2 * SIDE + inner) * 2 + source % 2) * UNIT
    outer = outer // 2

    total = jax.ShapeDtypeStruct((2 * PATCHES, heads), f32)
    summed, stats = call(
        first_kernel,
        "project_first",
        (total, jax.ShapeDtypeStruct((TAIL, heads), f32)),
        (starts, outer, *features, *pieces[:-2]),
        2,
        [pltpu.VMEM((FULL, 2 * PATCHES), bf16)],
        2 * 512 * 2592 * heads,
        6 * 2**20,
    )
    partial = jax.ShapeDtypeStruct((PATCHES + 8, heads), f32)
    mine, send = call(
        last_kernel,
        "project_last",
        (partial, partial),
        (starts, outer, core.reshape(1), *features, *pieces[-2:], summed, stats),
        3,
        [
            pltpu.VMEM((HALF + FULL, 2 * PATCHES), bf16),
            pltpu.VMEM((HALF + FULL, heads), bf16),
            pltpu.VMEM((2 * PATCHES, heads), f32),
        ],
        2 * 512 * 480 * heads,
        2 * 2**20,
    )
    received = to_sibling(send, pairs_z)

    group_row = jax.ShapeDtypeStruct((1, groups), f32)
    probs, old_weights = call(
        scores_kernel,
        "scores",
        (jax.ShapeDtypeStruct((heads // HD, PATCHES, PATCHES), f32), group_row),
        (queries, keys, group_weights.reshape(1, groups)),
        flops=2 * PATCHES * PATCHES * heads,
    )
    out = jax.ShapeDtypeStruct(queries.shape, bf16)
    query_grad, key_grad, value_grad, new_weights = call(
        attention_kernel,
        "attention",
        (out, out, out, group_row),
        (group_ids, mine, received, old_weights, probs, queries, keys, values),
        1,
        flops=8 * PATCHES * PATCHES * heads,
        moved=3 * 2**20,
    )
    return query_grad, key_grad, value_grad, new_weights.reshape(groups)


def solution(mesh):
    placed = (
        P("dp", "mp"),
        P("mp", "dp"),
        P("dp", "mp"),
        P("dp", "mp"),
        P("dp", "mp"),
        P("dp"),
        P("dp"),
        P(),
    )
    return jax.shard_map(
        functools.partial(per_device, mesh.shape["dp"] // 2),
        mesh=mesh,
        in_specs=placed,
        out_specs=(P("dp", "mp"), P("dp", "mp"), P("dp", "mp"), P()),
        check_vma=False,
    )
```

```python
import functools

import jax
import jax.numpy as jnp
from jax import lax
from jax.experimental import pallas as pl
from jax.experimental.pallas import tpu as pltpu
from jax.sharding import PartitionSpec as P

HD = 128
PATCHES = 256
ROBUST_RATE = 0.5
SIDE = 4
FAR = 8
UNIT = 96
STATS = 4
TAIL = 16
HALF = 2 * UNIT + TAIL
FULL = 4 * UNIT + TAIL
ALL = ("dp", "mp")


def along_z(x, step0, step1, pairs_z):
    pairs = [
        (2 * z + c, 2 * ((z + step) % pairs_z) + c)
        for z in range(pairs_z)
        for c, step in ((0, step0), (1, step1))
    ]
    return lax.ppermute(x, "dp", pairs)


def to_sibling(x, pairs_z):
    return lax.ppermute(x, "dp", [(i, i ^ 1) for i in range(2 * pairs_z)])


def exchange(x, flip, first_axis, pairs_z):
    pairs = []
    for d in range(2 * pairs_z):
        on_x = (d % 2 == 0) == first_axis
        for m in range(SIDE * SIDE):
            i, j = divmod(m, SIDE)
            to = (i ^ flip) * SIDE + j if on_x else i * SIDE + (j ^ flip)
            pairs.append((d * SIDE * SIDE + m, d * SIDE * SIDE + to))
    return lax.ppermute(x, ALL, pairs)


def gather(unit, block, pairs_z):
    mine = along_z(unit, FAR, -FAR, pairs_z)
    opposite = along_z(unit, -FAR, FAR, pairs_z)
    passed = exchange(block, 1, True, pairs_z)
    mine, opposite = meet(2, mine, opposite)
    farthest = along_z(mine, FAR, -FAR, pairs_z)
    block = stack([block, passed])
    passed = exchange(block, 3, True, pairs_z)
    (farthest,) = meet(4, farthest)
    bundle = join_units(unit, opposite, farthest, mine)
    block = stack([block, passed])
    pieces = [bundle]
    p = q = bundle
    for step, wait in enumerate((6, 6, 8)):
        p = along_z(p, 1, -1, pairs_z)
        q = along_z(q, -1, 1, pairs_z)
        if step < 2:
            passed = exchange(block, 1 + 2 * step, False, pairs_z)
        if step < 2:
            p, q = meet(wait, p, q)
        if step == 0:
            block = stack([block, passed])
        pieces += [p, q]
    half = passed
    p, q = cut(wait, p, q)
    p = along_z(p, 1, -1, pairs_z)
    q = along_z(q, -1, 1, pairs_z)
    return pieces + [p, q], [block, half]


def piece_offsets():
    slots = [0, FAR, 2 * FAR, -FAR]
    offsets = [slots]
    for k in range(1, FAR // 2):
        offsets += [[o - k for o in slots], [o + k for o in slots]]
    k = FAR // 2
    offsets += [[o - k for o in slots[:2]], [o + k for o in slots[1:3]]]
    return offsets


def unit_kernel(group, loss, weight_ref, unit_ref):
    heads = weight_ref.shape[1]
    unit_ref[pl.ds(0, UNIT), :] = weight_ref[...]
    x = jnp.full((TAIL, heads), loss[0], jnp.float32)
    high = x.astype(jnp.bfloat16).astype(jnp.float32)
    middle = (x - high).astype(jnp.bfloat16).astype(jnp.float32)
    low = x - high - middle
    row = lax.broadcasted_iota(jnp.int32, x.shape, 0)
    lane = lax.broadcasted_iota(jnp.int32, x.shape, 1)
    value = jnp.where(row == 0, 1.0, jnp.where(row == 1, high, jnp.where(row == 2, middle, low)))
    value = jnp.where((row < STATS) & (lane == group[0]), value, 0.0)
    unit_ref[pl.ds(UNIT, TAIL), :] = value.astype(jnp.bfloat16)


def join_kernel(*refs):
    *units, out = refs
    tail = jnp.zeros((TAIL, out.shape[1]), jnp.float32)
    for i, ref in enumerate(units):
        out[pl.ds(row_of(i), UNIT), :] = ref[pl.ds(0, UNIT), :]
        rows = ref[pl.ds(UNIT, TAIL), :].astype(jnp.float32)
        tail += pltpu.roll(rows, STATS * i, 0) if i else rows
    out[pl.ds(2 * UNIT, TAIL), :] = tail.astype(jnp.bfloat16)


def row_of(i):
    return i * UNIT + (TAIL if i >= 2 else 0)


def copy_kernel(*refs):
    half = len(refs) // 2
    for given, out in zip(refs[:half], refs[half:]):
        out[...] = given[...]


def cut_kernel(p_ref, q_ref, p_out, q_out, p_sem, q_sem):
    copies = (
        pltpu.make_async_copy(p_ref.at[pl.ds(0, HALF), :], p_out, p_sem),
        pltpu.make_async_copy(q_ref.at[pl.ds(UNIT, HALF), :], q_out, q_sem),
    )
    for copy in copies:
        copy.start()
    for copy in copies:
        copy.wait()


def stack_kernel(*refs):
    *blocks, out = refs
    rows = blocks[0].shape[0]
    for i, ref in enumerate(blocks):
        out[pl.ds(i * rows, rows), :] = ref[...]


def scores_kernel(q_ref, k_ref, gw_ref, probs_ref, weights_ref):
    weights_ref[...] = gw_ref[...]
    factor = 1.0 / jnp.sqrt(jnp.float32(HD))
    for h in range(q_ref.shape[1] // HD):
        cols = slice(h * HD, (h + 1) * HD)
        scores = lax.dot_general(
            q_ref[:, cols],
            k_ref[:, cols],
            (((1,), (1,)), ((), ())),
            preferred_element_type=jnp.float32,
        )
        raised = jnp.exp(scores * factor)
        probs_ref[h] = raised / jnp.sum(raised, axis=1, keepdims=True)


def pick_rows(starts, outers, slot, blocks, xs_ref, at):
    row = pl.multiple_of(starts[slot], 32)
    for i, block in enumerate(blocks):

        @pl.when(outers[slot] == i)
        def _():
            xs_ref[pl.ds(at, UNIT), :] = block[pl.ds(row, UNIT), :]


def product_of(xs, weight):
    return lax.dot_general(
        xs, weight, (((0,), (0,)), ((), ())), preferred_element_type=jnp.float32
    )


def first_kernel(starts, outers, *refs):
    blocks, pieces, (acc_ref, stats_ref, xs_ref) = refs[:2], refs[2:-3], refs[-3:]
    xs_ref[pl.ds(2 * UNIT, TAIL), :] = jnp.zeros((TAIL, xs_ref.shape[1]), xs_ref.dtype)
    stats_ref[...] = jnp.zeros_like(stats_ref)
    for i, piece in enumerate(pieces):
        for k in range(4):
            pick_rows(starts, outers, 4 * i + k, blocks, xs_ref, row_of(k))
        product = product_of(xs_ref[...], piece[...])
        if i == 0:
            acc_ref[...] = product
        else:
            acc_ref[...] += product
        stats_ref[...] += piece[pl.ds(2 * UNIT, TAIL), :].astype(jnp.float32)


def last_kernel(starts, outers, core, *refs):
    blocks, (p_ref, q_ref, acc_ref, stats_ref, mine_ref, send_ref, xs_ref, w_ref, sum_ref) = refs[:2], refs[2:]
    for k, at in enumerate((0, UNIT, HALF, HALF + UNIT + TAIL)):
        pick_rows(starts, outers, 28 + k, blocks, xs_ref, at)
    for at in (2 * UNIT, HALF + UNIT):
        xs_ref[pl.ds(at, TAIL), :] = jnp.zeros((TAIL, xs_ref.shape[1]), xs_ref.dtype)
    w_ref[pl.ds(0, HALF), :] = p_ref[...]
    w_ref[pl.ds(HALF, HALF), :] = q_ref[...]
    sum_ref[...] = acc_ref[...] + product_of(xs_ref[...], w_ref[...])
    stats = stats_ref[...]
    row = lax.broadcasted_iota(jnp.int32, stats.shape, 0)
    stats += jnp.where(row < 8, p_ref[pl.ds(2 * UNIT, TAIL), :].astype(jnp.float32), 0.0)
    middle = (row >= 4) & (row < 12)
    stats += jnp.where(middle, q_ref[pl.ds(UNIT, TAIL), :].astype(jnp.float32), 0.0)
    count = jnp.sum(jnp.where(row % 4 == 0, stats, 0.0), axis=0, keepdims=True)
    total = jnp.sum(jnp.where(row % 4 == 0, 0.0, stats), axis=0, keepdims=True)
    row8 = row[:8]
    tail = jnp.where(row8 == 0, count, jnp.where(row8 == 1, total, 0.0))
    here = pl.multiple_of(core[0] * PATCHES, PATCHES)
    there = pl.multiple_of((1 - core[0]) * PATCHES, PATCHES)
    mine_ref[pl.ds(0, PATCHES), :] = sum_ref[pl.ds(here, PATCHES), :]
    send_ref[pl.ds(0, PATCHES), :] = sum_ref[pl.ds(there, PATCHES), :]
    mine_ref[pl.ds(PATCHES, 8), :] = tail
    send_ref[pl.ds(PATCHES, 8), :] = tail


def attention_kernel(group, mine_ref, got_ref, gw_ref, probs_ref, q_ref, k_ref, v_ref, dq_ref, dk_ref, dv_ref, nw_ref):
    f32, bf16 = jnp.float32, jnp.bfloat16
    width = gw_ref.shape[1]
    tail = mine_ref[pl.ds(PATCHES, 8), :] + got_ref[pl.ds(PATCHES, 8), :]
    counts, totals = tail[0:1, :width], tail[1:2, :width]
    floored = jnp.maximum(counts, 1.0)
    raised = gw_ref[...] * jnp.exp(ROBUST_RATE * (totals / floored))
    new_weights = raised / jnp.sum(raised, axis=1, keepdims=True)
    nw_ref[...] = new_weights
    label = lax.broadcasted_iota(jnp.int32, (1, width), 1)
    scale = jnp.sum(
        jnp.where(label == group[0], new_weights / floored, 0.0), axis=1, keepdims=True
    )
    product = mine_ref[pl.ds(0, PATCHES), :] + got_ref[pl.ds(0, PATCHES), :]
    head_grad = (product * scale).astype(bf16)
    factor = 1.0 / jnp.sqrt(f32(HD))
    rows_by_rows = (((1,), (1,)), ((), ()))
    columns = (((0,), (0,)), ((), ()))
    plain = (((1,), (0,)), ((), ()))
    dot = functools.partial(lax.dot_general, preferred_element_type=f32)
    for h in range(q_ref.shape[1] // HD):
        cols = slice(h * HD, (h + 1) * HD)
        q, k, v, g = q_ref[:, cols], k_ref[:, cols], v_ref[:, cols], head_grad[:, cols]
        probs = probs_ref[h]
        dv_ref[:, cols] = dot(probs.astype(bf16), g, columns).astype(bf16)
        prob_grad = dot(g, v, rows_by_rows)
        centre = jnp.sum(probs * prob_grad, axis=1, keepdims=True)
        score = (probs * (prob_grad - centre)).astype(bf16)
        dq_ref[:, cols] = (dot(score, k, plain) * factor).astype(bf16)
        dk_ref[:, cols] = (dot(score, q, columns) * factor).astype(bf16)


VM = pl.BlockSpec(memory_space=pltpu.VMEM)
SM = pl.BlockSpec(memory_space=pltpu.SMEM)


def call(kernel, name, out_shape, operands, scalars=0, scratch=(), flops=0, moved=2**20):
    outs = jax.tree.map(lambda _: VM, out_shape)
    return pl.pallas_call(
        kernel,
        out_shape=out_shape,
        in_specs=[SM] * scalars + [VM] * (len(operands) - scalars),
        out_specs=outs,
        scratch_shapes=scratch,
        compiler_params=pltpu.CompilerParams(vmem_limit_bytes=16 * 2**20),
        cost_estimate=pl.CostEstimate(flops=flops, bytes_accessed=moved, transcendentals=0),
        name=name,
    )(*operands)


def join_units(*units):
    shape = jax.ShapeDtypeStruct((FULL, units[0].shape[1]), units[0].dtype)
    return call(join_kernel, "join_units", shape, units)


def meet(microseconds, *arrays):
    places = [pl.BlockSpec(memory_space=pl.ANY)] * len(arrays)
    return pl.pallas_call(
        lambda *refs: None,
        out_shape=tuple(jax.ShapeDtypeStruct(a.shape, a.dtype) for a in arrays),
        in_specs=places,
        out_specs=tuple(places),
        input_output_aliases={i: i for i in range(len(arrays))},
        compiler_params=pltpu.CompilerParams(vmem_limit_bytes=2**20),
        cost_estimate=pl.CostEstimate(
            flops=microseconds * 10**9, bytes_accessed=0, transcendentals=0
        ),
        name="meet",
    )(*arrays)


def cut(microseconds, p, q):
    shape = jax.ShapeDtypeStruct((HALF, p.shape[1]), p.dtype)
    return pl.pallas_call(
        cut_kernel,
        out_shape=(shape, shape),
        in_specs=[pl.BlockSpec(memory_space=pl.ANY)] * 2,
        out_specs=(VM, VM),
        scratch_shapes=[pltpu.SemaphoreType.DMA, pltpu.SemaphoreType.DMA],
        compiler_params=pltpu.CompilerParams(vmem_limit_bytes=4 * 2**20),
        cost_estimate=pl.CostEstimate(
            flops=microseconds * 10**9, bytes_accessed=0, transcendentals=0
        ),
        name="cut",
    )(p, q)


def stack(blocks):
    rows, width = blocks[0].shape
    shape = jax.ShapeDtypeStruct((len(blocks) * rows, width), blocks[0].dtype)
    return call(stack_kernel, "stack", shape, blocks)


def per_device(pairs_z, cotangent, out_weight, queries, keys, values, image_loss, group_ids, group_weights):
    f32, bf16 = jnp.float32, jnp.bfloat16
    groups = group_weights.shape[0]
    heads = queries.shape[1]
    core = lax.axis_index("dp") % 2
    first = core == 0
    z = lax.axis_index("dp") // 2
    mp = lax.axis_index("mp")
    at_x, at_y = mp // SIDE, mp % SIDE

    unit = call(
        unit_kernel,
        "make_unit",
        jax.ShapeDtypeStruct((UNIT + TAIL, heads), bf16),
        (group_ids, image_loss, out_weight.T),
        2,
        moved=2**17,
    )

    turned = cotangent.T.reshape(2, 2, UNIT, PATCHES)
    keep = jnp.where(first, turned[:, 0], turned[:, 1])
    give = jnp.where(first, turned[:, 1], turned[:, 0])
    got = to_sibling(give, pairs_z)
    block = jnp.concatenate([jnp.where(first, keep, got), jnp.where(first, got, keep)], axis=2)
    block = block.reshape(2 * UNIT, 2 * PATCHES)
    pieces, features = gather(unit, block, pairs_z)

    offsets = jnp.array([o for piece in piece_offsets() for o in piece], jnp.int32)
    source = (z + jnp.where(first, offsets, -offsets)) % pairs_z
    from_x, from_y = at_x ^ (source // 2 // SIDE), at_y ^ (source // 2 % SIDE)
    inner = jnp.where(first, from_x, from_y)
    outer = jnp.where(first, from_y, from_x)
    inner, outer = inner ^ (inner >> 1), outer ^ (outer >> 1)
    starts = ((outer % 2 * SIDE + inner) * 2 + source % 2) * UNIT
    outer = outer // 2

    total = jax.ShapeDtypeStruct((2 * PATCHES, heads), f32)
    summed, stats = call(
        first_kernel,
        "project_first",
        (total, jax.ShapeDtypeStruct((TAIL, heads), f32)),
        (starts, outer, *features, *pieces[:7]),
        2,
        [pltpu.VMEM((FULL, 2 * PATCHES), bf16)],
        2 * 512 * 2688 * heads,
        6 * 2**20,
    )
    partial = jax.ShapeDtypeStruct((PATCHES + 8, heads), f32)
    mine, send = call(
        last_kernel,
        "project_last",
        (partial, partial),
        (starts, outer, core.reshape(1), *features, *pieces[7:], summed, stats),
        3,
        [
            pltpu.VMEM((2 * HALF, 2 * PATCHES), bf16),
            pltpu.VMEM((2 * HALF, heads), bf16),
            pltpu.VMEM((2 * PATCHES, heads), f32),
        ],
        2 * 512 * 384 * heads,
        2 * 2**20,
    )
    received = to_sibling(send, pairs_z)

    group_row = jax.ShapeDtypeStruct((1, groups), f32)
    probs, old_weights = call(
        scores_kernel,
        "scores",
        (jax.ShapeDtypeStruct((heads // HD, PATCHES, PATCHES), f32), group_row),
        (queries, keys, group_weights.reshape(1, groups)),
        flops=2 * PATCHES * PATCHES * heads,
    )
    out = jax.ShapeDtypeStruct(queries.shape, bf16)
    query_grad, key_grad, value_grad, new_weights = call(
        attention_kernel,
        "attention",
        (out, out, out, group_row),
        (group_ids, mine, received, old_weights, probs, queries, keys, values),
        1,
        flops=8 * PATCHES * PATCHES * heads,
        moved=3 * 2**20,
    )
    return query_grad, key_grad, value_grad, new_weights.reshape(groups)


def solution(mesh):
    placed = (
        P("dp", "mp"),
        P("mp", "dp"),
        P("dp", "mp"),
        P("dp", "mp"),
        P("dp", "mp"),
        P("dp"),
        P("dp"),
        P(),
    )
    return jax.shard_map(
        functools.partial(per_device, mesh.shape["dp"] // 2),
        mesh=mesh,
        in_specs=placed,
        out_specs=(P("dp", "mp"), P("dp", "mp"), P("dp", "mp"), P()),
        check_vma=False,
    )
```

```python
import functools

import jax
import jax.numpy as jnp
from jax import lax
from jax.experimental import pallas as pl
from jax.experimental.pallas import tpu as pltpu
from jax.sharding import PartitionSpec as P

HD = 128
PATCHES = 256
ROBUST_RATE = 0.5
SIDE = 4
FAR = 8
UNIT = 96
STATS = 4
TAIL = 16
HALF = 2 * UNIT + TAIL
FULL = 4 * UNIT + TAIL
ALL = ("dp", "mp")


def along_z(x, step0, step1, pairs_z):
    pairs = [
        (2 * z + c, 2 * ((z + step) % pairs_z) + c)
        for z in range(pairs_z)
        for c, step in ((0, step0), (1, step1))
    ]
    return lax.ppermute(x, "dp", pairs)


def to_sibling(x, pairs_z):
    return lax.ppermute(x, "dp", [(i, i ^ 1) for i in range(2 * pairs_z)])


def exchange(x, flip, first_axis, pairs_z):
    pairs = []
    for d in range(2 * pairs_z):
        on_x = (d % 2 == 0) == first_axis
        for m in range(SIDE * SIDE):
            i, j = divmod(m, SIDE)
            to = (i ^ flip) * SIDE + j if on_x else i * SIDE + (j ^ flip)
            pairs.append((d * SIDE * SIDE + m, d * SIDE * SIDE + to))
    return lax.ppermute(x, ALL, pairs)


def gather(unit, block, pairs_z):
    mine = along_z(unit, FAR, -FAR, pairs_z)
    opposite = along_z(unit, -FAR, FAR, pairs_z)
    passed = exchange(block, 1, True, pairs_z)
    (mine,) = meet(2, mine)
    farthest = along_z(mine, FAR, -FAR, pairs_z)
    block = stack([block, passed])
    passed = exchange(block, 3, True, pairs_z)
    (opposite,) = meet(1, opposite)
    farthest, opposite = meet(4, farthest, opposite)
    bundle = join_units(unit, opposite, farthest, mine)
    block = stack([block, passed])
    pieces = [bundle]
    p = q = bundle
    for step, wait in enumerate((6, 6, 8)):
        p = along_z(p, 1, -1, pairs_z)
        q = along_z(q, -1, 1, pairs_z)
        if step < 2:
            passed = exchange(block, 1 + 2 * step, False, pairs_z)
        if step < 2:
            p, q = meet(wait, p, q)
        if step == 0:
            block = stack([block, passed])
        pieces += [p, q]
    half = passed
    p, q = cut(wait, p, q)
    p = along_z(p, 1, -1, pairs_z)
    q = along_z(q, -1, 1, pairs_z)
    return pieces + [p, q], [block, half]


def piece_offsets():
    slots = [0, FAR, 2 * FAR, -FAR]
    offsets = [slots]
    for k in range(1, FAR // 2):
        offsets += [[o - k for o in slots], [o + k for o in slots]]
    k = FAR // 2
    offsets += [[o - k for o in slots[:2]], [o + k for o in slots[1:3]]]
    return offsets


def unit_kernel(group, loss, weight_ref, unit_ref):
    heads = weight_ref.shape[1]
    unit_ref[pl.ds(0, UNIT), :] = weight_ref[...]
    x = jnp.full((TAIL, heads), loss[0], jnp.float32)
    high = x.astype(jnp.bfloat16).astype(jnp.float32)
    middle = (x - high).astype(jnp.bfloat16).astype(jnp.float32)
    low = x - high - middle
    row = lax.broadcasted_iota(jnp.int32, x.shape, 0)
    lane = lax.broadcasted_iota(jnp.int32, x.shape, 1)
    value = jnp.where(row == 0, 1.0, jnp.where(row == 1, high, jnp.where(row == 2, middle, low)))
    value = jnp.where((row < STATS) & (lane == group[0]), value, 0.0)
    unit_ref[pl.ds(UNIT, TAIL), :] = value.astype(jnp.bfloat16)


def join_kernel(*refs):
    *units, out = refs
    tail = jnp.zeros((TAIL, out.shape[1]), jnp.float32)
    for i, ref in enumerate(units):
        out[pl.ds(row_of(i), UNIT), :] = ref[pl.ds(0, UNIT), :]
        rows = ref[pl.ds(UNIT, TAIL), :].astype(jnp.float32)
        tail += pltpu.roll(rows, STATS * i, 0) if i else rows
    out[pl.ds(2 * UNIT, TAIL), :] = tail.astype(jnp.bfloat16)


def row_of(i):
    return i * UNIT + (TAIL if i >= 2 else 0)


def copy_kernel(*refs):
    half = len(refs) // 2
    for given, out in zip(refs[:half], refs[half:]):
        out[...] = given[...]


def cut_kernel(p_ref, q_ref, p_out, q_out, p_sem, q_sem):
    copies = (
        pltpu.make_async_copy(p_ref.at[pl.ds(0, HALF), :], p_out, p_sem),
        pltpu.make_async_copy(q_ref.at[pl.ds(UNIT, HALF), :], q_out, q_sem),
    )
    for copy in copies:
        copy.start()
    for copy in copies:
        copy.wait()


def stack_kernel(*refs):
    *blocks, out = refs
    rows = blocks[0].shape[0]
    for i, ref in enumerate(blocks):
        out[pl.ds(i * rows, rows), :] = ref[...]


def scores_kernel(q_ref, k_ref, gw_ref, probs_ref, weights_ref):
    weights_ref[...] = gw_ref[...]
    factor = 1.0 / jnp.sqrt(jnp.float32(HD))
    for h in range(q_ref.shape[1] // HD):
        cols = slice(h * HD, (h + 1) * HD)
        scores = lax.dot_general(
            q_ref[:, cols],
            k_ref[:, cols],
            (((1,), (1,)), ((), ())),
            preferred_element_type=jnp.float32,
        )
        raised = jnp.exp(scores * factor)
        probs_ref[h] = raised / jnp.sum(raised, axis=1, keepdims=True)


def pick_rows(starts, outers, slot, blocks, xs_ref, at):
    row = pl.multiple_of(starts[slot], 32)
    for i, block in enumerate(blocks):

        @pl.when(outers[slot] == i)
        def _():
            xs_ref[pl.ds(at, UNIT), :] = block[pl.ds(row, UNIT), :]


def product_of(xs, weight):
    return lax.dot_general(
        xs, weight, (((0,), (0,)), ((), ())), preferred_element_type=jnp.float32
    )


def first_kernel(starts, outers, *refs):
    blocks, pieces, (acc_ref, stats_ref, xs_ref) = refs[:2], refs[2:-3], refs[-3:]
    xs_ref[pl.ds(2 * UNIT, TAIL), :] = jnp.zeros((TAIL, xs_ref.shape[1]), xs_ref.dtype)
    stats_ref[...] = jnp.zeros_like(stats_ref)
    for i, piece in enumerate(pieces):
        for k in range(4):
            pick_rows(starts, outers, 4 * i + k, blocks, xs_ref, row_of(k))
        product = product_of(xs_ref[...], piece[...])
        if i == 0:
            acc_ref[...] = product
        else:
            acc_ref[...] += product
        stats_ref[...] += piece[pl.ds(2 * UNIT, TAIL), :].astype(jnp.float32)


def last_kernel(starts, outers, core, *refs):
    blocks, (p_ref, q_ref, acc_ref, stats_ref, mine_ref, send_ref, xs_ref, w_ref, sum_ref) = refs[:2], refs[2:]
    for k, at in enumerate((0, UNIT, HALF, HALF + UNIT + TAIL)):
        pick_rows(starts, outers, 28 + k, blocks, xs_ref, at)
    for at in (2 * UNIT, HALF + UNIT):
        xs_ref[pl.ds(at, TAIL), :] = jnp.zeros((TAIL, xs_ref.shape[1]), xs_ref.dtype)
    w_ref[pl.ds(0, HALF), :] = p_ref[...]
    w_ref[pl.ds(HALF, HALF), :] = q_ref[...]
    sum_ref[...] = acc_ref[...] + product_of(xs_ref[...], w_ref[...])
    stats = stats_ref[...]
    row = lax.broadcasted_iota(jnp.int32, stats.shape, 0)
    stats += jnp.where(row < 8, p_ref[pl.ds(2 * UNIT, TAIL), :].astype(jnp.float32), 0.0)
    middle = (row >= 4) & (row < 12)
    stats += jnp.where(middle, q_ref[pl.ds(UNIT, TAIL), :].astype(jnp.float32), 0.0)
    count = jnp.sum(jnp.where(row % 4 == 0, stats, 0.0), axis=0, keepdims=True)
    total = jnp.sum(jnp.where(row % 4 == 0, 0.0, stats), axis=0, keepdims=True)
    row8 = row[:8]
    tail = jnp.where(row8 == 0, count, jnp.where(row8 == 1, total, 0.0))
    here = pl.multiple_of(core[0] * PATCHES, PATCHES)
    there = pl.multiple_of((1 - core[0]) * PATCHES, PATCHES)
    mine_ref[pl.ds(0, PATCHES), :] = sum_ref[pl.ds(here, PATCHES), :]
    send_ref[pl.ds(0, PATCHES), :] = sum_ref[pl.ds(there, PATCHES), :]
    mine_ref[pl.ds(PATCHES, 8), :] = tail
    send_ref[pl.ds(PATCHES, 8), :] = tail


def attention_kernel(group, mine_ref, got_ref, gw_ref, probs_ref, q_ref, k_ref, v_ref, dq_ref, dk_ref, dv_ref, nw_ref):
    f32, bf16 = jnp.float32, jnp.bfloat16
    width = gw_ref.shape[1]
    tail = mine_ref[pl.ds(PATCHES, 8), :] + got_ref[pl.ds(PATCHES, 8), :]
    counts, totals = tail[0:1, :width], tail[1:2, :width]
    floored = jnp.maximum(counts, 1.0)
    raised = gw_ref[...] * jnp.exp(ROBUST_RATE * (totals / floored))
    new_weights = raised / jnp.sum(raised, axis=1, keepdims=True)
    nw_ref[...] = new_weights
    label = lax.broadcasted_iota(jnp.int32, (1, width), 1)
    scale = jnp.sum(
        jnp.where(label == group[0], new_weights / floored, 0.0), axis=1, keepdims=True
    )
    product = mine_ref[pl.ds(0, PATCHES), :] + got_ref[pl.ds(0, PATCHES), :]
    head_grad = (product * scale).astype(bf16)
    factor = 1.0 / jnp.sqrt(f32(HD))
    rows_by_rows = (((1,), (1,)), ((), ()))
    columns = (((0,), (0,)), ((), ()))
    plain = (((1,), (0,)), ((), ()))
    dot = functools.partial(lax.dot_general, preferred_element_type=f32)
    for h in range(q_ref.shape[1] // HD):
        cols = slice(h * HD, (h + 1) * HD)
        q, k, v, g = q_ref[:, cols], k_ref[:, cols], v_ref[:, cols], head_grad[:, cols]
        probs = probs_ref[h]
        dv_ref[:, cols] = dot(probs.astype(bf16), g, columns).astype(bf16)
        prob_grad = dot(g, v, rows_by_rows)
        centre = jnp.sum(probs * prob_grad, axis=1, keepdims=True)
        score = (probs * (prob_grad - centre)).astype(bf16)
        dq_ref[:, cols] = (dot(score, k, plain) * factor).astype(bf16)
        dk_ref[:, cols] = (dot(score, q, columns) * factor).astype(bf16)


VM = pl.BlockSpec(memory_space=pltpu.VMEM)
SM = pl.BlockSpec(memory_space=pltpu.SMEM)


def call(kernel, name, out_shape, operands, scalars=0, scratch=(), flops=0, moved=2**20):
    outs = jax.tree.map(lambda _: VM, out_shape)
    return pl.pallas_call(
        kernel,
        out_shape=out_shape,
        in_specs=[SM] * scalars + [VM] * (len(operands) - scalars),
        out_specs=outs,
        scratch_shapes=scratch,
        compiler_params=pltpu.CompilerParams(vmem_limit_bytes=16 * 2**20),
        cost_estimate=pl.CostEstimate(flops=flops, bytes_accessed=moved, transcendentals=0),
        name=name,
    )(*operands)


def join_units(*units):
    shape = jax.ShapeDtypeStruct((FULL, units[0].shape[1]), units[0].dtype)
    return call(join_kernel, "join_units", shape, units)


def meet(microseconds, *arrays):
    places = [pl.BlockSpec(memory_space=pl.ANY)] * len(arrays)
    return pl.pallas_call(
        lambda *refs: None,
        out_shape=tuple(jax.ShapeDtypeStruct(a.shape, a.dtype) for a in arrays),
        in_specs=places,
        out_specs=tuple(places),
        input_output_aliases={i: i for i in range(len(arrays))},
        compiler_params=pltpu.CompilerParams(vmem_limit_bytes=2**20),
        cost_estimate=pl.CostEstimate(
            flops=microseconds * 10**9, bytes_accessed=0, transcendentals=0
        ),
        name="meet",
    )(*arrays)


def cut(microseconds, p, q):
    shape = jax.ShapeDtypeStruct((HALF, p.shape[1]), p.dtype)
    return pl.pallas_call(
        cut_kernel,
        out_shape=(shape, shape),
        in_specs=[pl.BlockSpec(memory_space=pl.ANY)] * 2,
        out_specs=(VM, VM),
        scratch_shapes=[pltpu.SemaphoreType.DMA, pltpu.SemaphoreType.DMA],
        compiler_params=pltpu.CompilerParams(vmem_limit_bytes=4 * 2**20),
        cost_estimate=pl.CostEstimate(
            flops=microseconds * 10**9, bytes_accessed=0, transcendentals=0
        ),
        name="cut",
    )(p, q)


def stack(blocks):
    rows, width = blocks[0].shape
    shape = jax.ShapeDtypeStruct((len(blocks) * rows, width), blocks[0].dtype)
    return call(stack_kernel, "stack", shape, blocks)


def per_device(pairs_z, cotangent, out_weight, queries, keys, values, image_loss, group_ids, group_weights):
    f32, bf16 = jnp.float32, jnp.bfloat16
    groups = group_weights.shape[0]
    heads = queries.shape[1]
    core = lax.axis_index("dp") % 2
    first = core == 0
    z = lax.axis_index("dp") // 2
    mp = lax.axis_index("mp")
    at_x, at_y = mp // SIDE, mp % SIDE

    unit = call(
        unit_kernel,
        "make_unit",
        jax.ShapeDtypeStruct((UNIT + TAIL, heads), bf16),
        (group_ids, image_loss, out_weight.T),
        2,
        moved=2**17,
    )

    turned = cotangent.T.reshape(2, 2, UNIT, PATCHES)
    keep = jnp.where(first, turned[:, 0], turned[:, 1])
    give = jnp.where(first, turned[:, 1], turned[:, 0])
    got = to_sibling(give, pairs_z)
    block = jnp.concatenate([jnp.where(first, keep, got), jnp.where(first, got, keep)], axis=2)
    block = block.reshape(2 * UNIT, 2 * PATCHES)
    pieces, features = gather(unit, block, pairs_z)

    offsets = jnp.array([o for piece in piece_offsets() for o in piece], jnp.int32)
    source = (z + jnp.where(first, offsets, -offsets)) % pairs_z
    from_x, from_y = at_x ^ (source // 2 // SIDE), at_y ^ (source // 2 % SIDE)
    inner = jnp.where(first, from_x, from_y)
    outer = jnp.where(first, from_y, from_x)
    inner, outer = inner ^ (inner >> 1), outer ^ (outer >> 1)
    starts = ((outer % 2 * SIDE + inner) * 2 + source % 2) * UNIT
    outer = outer // 2

    total = jax.ShapeDtypeStruct((2 * PATCHES, heads), f32)
    summed, stats = call(
        first_kernel,
        "project_first",
        (total, jax.ShapeDtypeStruct((TAIL, heads), f32)),
        (starts, outer, *features, *pieces[:7]),
        2,
        [pltpu.VMEM((FULL, 2 * PATCHES), bf16)],
        2 * 512 * 2688 * heads,
        6 * 2**20,
    )
    partial = jax.ShapeDtypeStruct((PATCHES + 8, heads), f32)
    mine, send = call(
        last_kernel,
        "project_last",
        (partial, partial),
        (starts, outer, core.reshape(1), *features, *pieces[7:], summed, stats),
        3,
        [
            pltpu.VMEM((2 * HALF, 2 * PATCHES), bf16),
            pltpu.VMEM((2 * HALF, heads), bf16),
            pltpu.VMEM((2 * PATCHES, heads), f32),
        ],
        2 * 512 * 384 * heads,
        2 * 2**20,
    )
    received = to_sibling(send, pairs_z)

    group_row = jax.ShapeDtypeStruct((1, groups), f32)
    probs, old_weights = call(
        scores_kernel,
        "scores",
        (jax.ShapeDtypeStruct((heads // HD, PATCHES, PATCHES), f32), group_row),
        (queries, keys, group_weights.reshape(1, groups)),
        flops=2 * PATCHES * PATCHES * heads,
    )
    out = jax.ShapeDtypeStruct(queries.shape, bf16)
    query_grad, key_grad, value_grad, new_weights = call(
        attention_kernel,
        "attention",
        (out, out, out, group_row),
        (group_ids, mine, received, old_weights, probs, queries, keys, values),
        1,
        flops=8 * PATCHES * PATCHES * heads,
        moved=3 * 2**20,
    )
    return query_grad, key_grad, value_grad, new_weights.reshape(groups)


def solution(mesh):
    placed = (
        P("dp", "mp"),
        P("mp", "dp"),
        P("dp", "mp"),
        P("dp", "mp"),
        P("dp", "mp"),
        P("dp"),
        P("dp"),
        P(),
    )
    return jax.shard_map(
        functools.partial(per_device, mesh.shape["dp"] // 2),
        mesh=mesh,
        in_specs=placed,
        out_specs=(P("dp", "mp"), P("dp", "mp"), P("dp", "mp"), P()),
        check_vma=False,
    )
```

```python
import functools

import jax
import jax.numpy as jnp
from jax import lax
from jax.experimental import pallas as pl
from jax.experimental.pallas import tpu as pltpu
from jax.sharding import PartitionSpec as P

HD = 128
PATCHES = 256
ROBUST_RATE = 0.5
SIDE = 4
FAR = 8
UNIT = 96
STATS = 4
TAIL = 16
HALF = 2 * UNIT + TAIL
FULL = 4 * UNIT + TAIL
ALL = ("dp", "mp")


def along_z(x, step0, step1, pairs_z):
    pairs = [
        (2 * z + c, 2 * ((z + step) % pairs_z) + c)
        for z in range(pairs_z)
        for c, step in ((0, step0), (1, step1))
    ]
    return lax.ppermute(x, "dp", pairs)


def to_sibling(x, pairs_z):
    return lax.ppermute(x, "dp", [(i, i ^ 1) for i in range(2 * pairs_z)])


def exchange(x, flip, first_axis, pairs_z):
    pairs = []
    for d in range(2 * pairs_z):
        on_x = (d % 2 == 0) == first_axis
        for m in range(SIDE * SIDE):
            i, j = divmod(m, SIDE)
            to = (i ^ flip) * SIDE + j if on_x else i * SIDE + (j ^ flip)
            pairs.append((d * SIDE * SIDE + m, d * SIDE * SIDE + to))
    return lax.ppermute(x, ALL, pairs)


def gather(unit, block, pairs_z):
    mine = along_z(unit, FAR, -FAR, pairs_z)
    opposite = along_z(unit, -FAR, FAR, pairs_z)
    passed = exchange(block, 1, True, pairs_z)
    (mine,) = meet(2, mine)
    farthest = along_z(mine, FAR, -FAR, pairs_z)
    block = stack([block, passed])
    passed = exchange(block, 3, True, pairs_z)
    (opposite,) = meet(1, opposite)
    farthest, opposite = meet(4, farthest, opposite)
    bundle = join_units(unit, opposite, farthest, mine)
    block = stack([block, passed])
    pieces = [bundle]
    p = q = bundle
    for step, wait in enumerate((6, 6, 8)):
        p = along_z(p, 1, -1, pairs_z)
        q = along_z(q, -1, 1, pairs_z)
        if step < 2:
            passed = exchange(block, 1 + 2 * step, False, pairs_z)
        if step < 2:
            p, q = meet(wait, p, q)
        if step == 0:
            block = stack([block, passed])
        pieces += [p, q]
    half = passed
    p, q = cut(wait, p, q)
    p = along_z(p, 1, -1, pairs_z)
    q = along_z(q, -1, 1, pairs_z)
    return pieces + [p, q], [block, half]


def piece_offsets():
    slots = [0, FAR, 2 * FAR, -FAR]
    offsets = [slots]
    for k in range(1, FAR // 2):
        offsets += [[o - k for o in slots], [o + k for o in slots]]
    k = FAR // 2
    offsets += [[o - k for o in slots[:2]], [o + k for o in slots[1:3]]]
    return offsets


def unit_kernel(group, loss, weight_ref, unit_ref):
    heads = weight_ref.shape[1]
    unit_ref[pl.ds(0, UNIT), :] = weight_ref[...]
    x = jnp.broadcast_to(loss[...], (TAIL, heads))
    high = x.astype(jnp.bfloat16).astype(jnp.float32)
    middle = (x - high).astype(jnp.bfloat16).astype(jnp.float32)
    low = x - high - middle
    row = lax.broadcasted_iota(jnp.int32, x.shape, 0)
    lane = lax.broadcasted_iota(jnp.int32, x.shape, 1)
    value = jnp.where(row == 0, 1.0, jnp.where(row == 1, high, jnp.where(row == 2, middle, low)))
    value = jnp.where((row < STATS) & (lane == group[...]), value, 0.0)
    unit_ref[pl.ds(UNIT, TAIL), :] = value.astype(jnp.bfloat16)


def join_kernel(*refs):
    *units, out = refs
    tail = jnp.zeros((TAIL, out.shape[1]), jnp.float32)
    for i, ref in enumerate(units):
        out[pl.ds(row_of(i), UNIT), :] = ref[pl.ds(0, UNIT), :]
        rows = ref[pl.ds(UNIT, TAIL), :].astype(jnp.float32)
        tail += pltpu.roll(rows, STATS * i, 0) if i else rows
    out[pl.ds(2 * UNIT, TAIL), :] = tail.astype(jnp.bfloat16)


def row_of(i):
    return i * UNIT + (TAIL if i >= 2 else 0)


def copy_kernel(*refs):
    half = len(refs) // 2
    for given, out in zip(refs[:half], refs[half:]):
        out[...] = given[...]


def cut_kernel(p_ref, q_ref, p_out, q_out, p_sem, q_sem):
    copies = (
        pltpu.make_async_copy(p_ref.at[pl.ds(0, HALF), :], p_out, p_sem),
        pltpu.make_async_copy(q_ref.at[pl.ds(UNIT, HALF), :], q_out, q_sem),
    )
    for copy in copies:
        copy.start()
    for copy in copies:
        copy.wait()


def stack_kernel(*refs):
    *blocks, out = refs
    rows = blocks[0].shape[0]
    for i, ref in enumerate(blocks):
        out[pl.ds(i * rows, rows), :] = ref[...]


def scores_kernel(q_ref, k_ref, gw_ref, probs_ref, weights_ref):
    weights_ref[...] = gw_ref[...]
    factor = 1.0 / jnp.sqrt(jnp.float32(HD))
    for h in range(q_ref.shape[1] // HD):
        cols = slice(h * HD, (h + 1) * HD)
        scores = lax.dot_general(
            q_ref[:, cols],
            k_ref[:, cols],
            (((1,), (1,)), ((), ())),
            preferred_element_type=jnp.float32,
        )
        raised = jnp.exp(scores * factor)
        probs_ref[h] = raised / jnp.sum(raised, axis=1, keepdims=True)


def pick_rows(starts, outers, slot, blocks, xs_ref, at):
    row = pl.multiple_of(starts[slot], 32)
    for i, block in enumerate(blocks):

        @pl.when(outers[slot] == i)
        def _():
            xs_ref[pl.ds(at, UNIT), :] = block[pl.ds(row, UNIT), :]


def product_of(xs, weight):
    return lax.dot_general(
        xs, weight, (((0,), (0,)), ((), ())), preferred_element_type=jnp.float32
    )


def first_kernel(starts, outers, *refs):
    blocks, pieces, (acc_ref, stats_ref, xs_ref) = refs[:2], refs[2:-3], refs[-3:]
    xs_ref[pl.ds(2 * UNIT, TAIL), :] = jnp.zeros((TAIL, xs_ref.shape[1]), xs_ref.dtype)
    stats_ref[...] = jnp.zeros_like(stats_ref)
    for i, piece in enumerate(pieces):
        for k in range(4):
            pick_rows(starts, outers, 4 * i + k, blocks, xs_ref, row_of(k))
        product = product_of(xs_ref[...], piece[...])
        if i == 0:
            acc_ref[...] = product
        else:
            acc_ref[...] += product
        stats_ref[...] += piece[pl.ds(2 * UNIT, TAIL), :].astype(jnp.float32)


def last_kernel(starts, outers, core, *refs):
    blocks, (p_ref, q_ref, acc_ref, stats_ref, mine_ref, send_ref, xs_ref, w_ref, sum_ref) = refs[:2], refs[2:]
    for k, at in enumerate((0, UNIT, HALF, HALF + UNIT + TAIL)):
        pick_rows(starts, outers, 28 + k, blocks, xs_ref, at)
    for at in (2 * UNIT, HALF + UNIT):
        xs_ref[pl.ds(at, TAIL), :] = jnp.zeros((TAIL, xs_ref.shape[1]), xs_ref.dtype)
    w_ref[pl.ds(0, HALF), :] = p_ref[...]
    w_ref[pl.ds(HALF, HALF), :] = q_ref[...]
    sum_ref[...] = acc_ref[...] + product_of(xs_ref[...], w_ref[...])
    stats = stats_ref[...]
    row = lax.broadcasted_iota(jnp.int32, stats.shape, 0)
    stats += jnp.where(row < 8, p_ref[pl.ds(2 * UNIT, TAIL), :].astype(jnp.float32), 0.0)
    middle = (row >= 4) & (row < 12)
    stats += jnp.where(middle, q_ref[pl.ds(UNIT, TAIL), :].astype(jnp.float32), 0.0)
    count = jnp.sum(jnp.where(row % 4 == 0, stats, 0.0), axis=0, keepdims=True)
    total = jnp.sum(jnp.where(row % 4 == 0, 0.0, stats), axis=0, keepdims=True)
    row8 = row[:8]
    tail = jnp.where(row8 == 0, count, jnp.where(row8 == 1, total, 0.0))
    here = pl.multiple_of(core[0] * PATCHES, PATCHES)
    there = pl.multiple_of((1 - core[0]) * PATCHES, PATCHES)
    mine_ref[pl.ds(0, PATCHES), :] = sum_ref[pl.ds(here, PATCHES), :]
    send_ref[pl.ds(0, PATCHES), :] = sum_ref[pl.ds(there, PATCHES), :]
    mine_ref[pl.ds(PATCHES, 8), :] = tail
    send_ref[pl.ds(PATCHES, 8), :] = tail


def attention_kernel(group, mine_ref, got_ref, gw_ref, probs_ref, q_ref, k_ref, v_ref, dq_ref, dk_ref, dv_ref, nw_ref):
    f32, bf16 = jnp.float32, jnp.bfloat16
    width = gw_ref.shape[1]
    tail = mine_ref[pl.ds(PATCHES, 8), :] + got_ref[pl.ds(PATCHES, 8), :]
    counts, totals = tail[0:1, :width], tail[1:2, :width]
    floored = jnp.maximum(counts, 1.0)
    raised = gw_ref[...] * jnp.exp(ROBUST_RATE * (totals / floored))
    new_weights = raised / jnp.sum(raised, axis=1, keepdims=True)
    nw_ref[...] = new_weights
    label = lax.broadcasted_iota(jnp.int32, (1, width), 1)
    scale = jnp.sum(
        jnp.where(label == group[...], new_weights / floored, 0.0), axis=1, keepdims=True
    )
    product = mine_ref[pl.ds(0, PATCHES), :] + got_ref[pl.ds(0, PATCHES), :]
    head_grad = (product * scale).astype(bf16)
    factor = 1.0 / jnp.sqrt(f32(HD))
    rows_by_rows = (((1,), (1,)), ((), ()))
    columns = (((0,), (0,)), ((), ()))
    plain = (((1,), (0,)), ((), ()))
    dot = functools.partial(lax.dot_general, preferred_element_type=f32)
    for h in range(q_ref.shape[1] // HD):
        cols = slice(h * HD, (h + 1) * HD)
        q, k, v, g = q_ref[:, cols], k_ref[:, cols], v_ref[:, cols], head_grad[:, cols]
        probs = probs_ref[h]
        dv_ref[:, cols] = dot(probs.astype(bf16), g, columns).astype(bf16)
        prob_grad = dot(g, v, rows_by_rows)
        centre = jnp.sum(probs * prob_grad, axis=1, keepdims=True)
        score = (probs * (prob_grad - centre)).astype(bf16)
        dq_ref[:, cols] = (dot(score, k, plain) * factor).astype(bf16)
        dk_ref[:, cols] = (dot(score, q, columns) * factor).astype(bf16)


VM = pl.BlockSpec(memory_space=pltpu.VMEM)
SM = pl.BlockSpec(memory_space=pltpu.SMEM)


def call(kernel, name, out_shape, operands, scalars=0, scratch=(), flops=0, moved=2**20):
    outs = jax.tree.map(lambda _: VM, out_shape)
    return pl.pallas_call(
        kernel,
        out_shape=out_shape,
        in_specs=[SM] * scalars + [VM] * (len(operands) - scalars),
        out_specs=outs,
        scratch_shapes=scratch,
        compiler_params=pltpu.CompilerParams(vmem_limit_bytes=16 * 2**20),
        cost_estimate=pl.CostEstimate(flops=flops, bytes_accessed=moved, transcendentals=0),
        name=name,
    )(*operands)


def join_units(*units):
    shape = jax.ShapeDtypeStruct((FULL, units[0].shape[1]), units[0].dtype)
    return call(join_kernel, "join_units", shape, units)


def meet(microseconds, *arrays):
    places = [pl.BlockSpec(memory_space=pl.ANY)] * len(arrays)
    return pl.pallas_call(
        lambda *refs: None,
        out_shape=tuple(jax.ShapeDtypeStruct(a.shape, a.dtype) for a in arrays),
        in_specs=places,
        out_specs=tuple(places),
        input_output_aliases={i: i for i in range(len(arrays))},
        compiler_params=pltpu.CompilerParams(vmem_limit_bytes=2**20),
        cost_estimate=pl.CostEstimate(
            flops=microseconds * 10**9, bytes_accessed=0, transcendentals=0
        ),
        name="meet",
    )(*arrays)


def cut(microseconds, p, q):
    shape = jax.ShapeDtypeStruct((HALF, p.shape[1]), p.dtype)
    return pl.pallas_call(
        cut_kernel,
        out_shape=(shape, shape),
        in_specs=[pl.BlockSpec(memory_space=pl.ANY)] * 2,
        out_specs=(VM, VM),
        scratch_shapes=[pltpu.SemaphoreType.DMA, pltpu.SemaphoreType.DMA],
        compiler_params=pltpu.CompilerParams(vmem_limit_bytes=4 * 2**20),
        cost_estimate=pl.CostEstimate(
            flops=microseconds * 10**9, bytes_accessed=0, transcendentals=0
        ),
        name="cut",
    )(p, q)


def stack(blocks):
    rows, width = blocks[0].shape
    shape = jax.ShapeDtypeStruct((len(blocks) * rows, width), blocks[0].dtype)
    return call(stack_kernel, "stack", shape, blocks)


def per_device(pairs_z, cotangent, out_weight, queries, keys, values, image_loss, group_ids, group_weights):
    f32, bf16 = jnp.float32, jnp.bfloat16
    groups = group_weights.shape[0]
    heads = queries.shape[1]
    core = lax.axis_index("dp") % 2
    first = core == 0
    z = lax.axis_index("dp") // 2
    mp = lax.axis_index("mp")
    at_x, at_y = mp // SIDE, mp % SIDE

    group = group_ids.reshape(1, 1)

    unit = call(
        unit_kernel,
        "make_unit",
        jax.ShapeDtypeStruct((UNIT + TAIL, heads), bf16),
        (group, image_loss.reshape(1, 1), out_weight.T),
        moved=2**17,
    )

    turned = cotangent.T.reshape(2, 2, UNIT, PATCHES)
    keep = jnp.where(first, turned[:, 0], turned[:, 1])
    give = jnp.where(first, turned[:, 1], turned[:, 0])
    got = to_sibling(give, pairs_z)
    block = jnp.concatenate([jnp.where(first, keep, got), jnp.where(first, got, keep)], axis=2)
    block = block.reshape(2 * UNIT, 2 * PATCHES)
    pieces, features = gather(unit, block, pairs_z)

    offsets = jnp.array([o for piece in piece_offsets() for o in piece], jnp.int32)
    source = (z + jnp.where(first, offsets, -offsets)) % pairs_z
    from_x, from_y = at_x ^ (source // 2 // SIDE), at_y ^ (source // 2 % SIDE)
    inner = jnp.where(first, from_x, from_y)
    outer = jnp.where(first, from_y, from_x)
    inner, outer = inner ^ (inner >> 1), outer ^ (outer >> 1)
    starts = ((outer % 2 * SIDE + inner) * 2 + source % 2) * UNIT
    outer = outer // 2

    total = jax.ShapeDtypeStruct((2 * PATCHES, heads), f32)
    summed, stats = call(
        first_kernel,
        "project_first",
        (total, jax.ShapeDtypeStruct((TAIL, heads), f32)),
        (starts, outer, *features, *pieces[:7]),
        2,
        [pltpu.VMEM((FULL, 2 * PATCHES), bf16)],
        2 * 512 * 2688 * heads,
        6 * 2**20,
    )
    partial = jax.ShapeDtypeStruct((PATCHES + 8, heads), f32)
    mine, send = call(
        last_kernel,
        "project_last",
        (partial, partial),
        (starts, outer, core.reshape(1), *features, *pieces[7:], summed, stats),
        3,
        [
            pltpu.VMEM((2 * HALF, 2 * PATCHES), bf16),
            pltpu.VMEM((2 * HALF, heads), bf16),
            pltpu.VMEM((2 * PATCHES, heads), f32),
        ],
        2 * 512 * 384 * heads,
        2 * 2**20,
    )
    received = to_sibling(send, pairs_z)

    group_row = jax.ShapeDtypeStruct((1, groups), f32)
    probs, old_weights = call(
        scores_kernel,
        "scores",
        (jax.ShapeDtypeStruct((heads // HD, PATCHES, PATCHES), f32), group_row),
        (queries, keys, group_weights.reshape(1, groups)),
        flops=2 * PATCHES * PATCHES * heads,
    )
    out = jax.ShapeDtypeStruct(queries.shape, bf16)
    query_grad, key_grad, value_grad, new_weights = call(
        attention_kernel,
        "attention",
        (out, out, out, group_row),
        (group, mine, received, old_weights, probs, queries, keys, values),
        flops=8 * PATCHES * PATCHES * heads,
        moved=3 * 2**20,
    )
    return query_grad, key_grad, value_grad, new_weights.reshape(groups)


def solution(mesh):
    placed = (
        P("dp", "mp"),
        P("mp", "dp"),
        P("dp", "mp"),
        P("dp", "mp"),
        P("dp", "mp"),
        P("dp"),
        P("dp"),
        P(),
    )
    return jax.shard_map(
        functools.partial(per_device, mesh.shape["dp"] // 2),
        mesh=mesh,
        in_specs=placed,
        out_specs=(P("dp", "mp"), P("dp", "mp"), P("dp", "mp"), P()),
        check_vma=False,
    )
```
